128 devices in a mesh: dp: 4 (over x), seq: 32 (over z, y, core).
Axes of the slice: x: 4, y: 4, z: 4, core: 2. Of those that a mesh axis runs over, the one named last changes fastest.
Arguments:
- inputs: bfloat16 [4, 4096, 960], P('dp', 'seq'), may hold values from -6 to 6
- w_project: bfloat16 [2, 960, 1600], P(None, 'dp', 'seq'), may hold values from -0.1875 to 0.1875
- w_output: bfloat16 [2, 960, 960], P(None, 'dp', 'seq'), may hold values from -1.5 to 1.5
- w_expand: bfloat16 [2, 960, 5120], P(None, 'dp', 'seq'), may hold values from -0.1875 to 0.1875
- w_contract: bfloat16 [2, 2560, 960], P(None, 'dp', 'seq'), may hold values from -0.125 to 0.125
- norm_gains: bfloat16 [3840], P(('dp', 'seq')), may hold values from 0.5 to 1.5
- segments: int32 [4, 4096], P('dp', 'seq'), may hold values from 0 to 20, as said below
- cotangent: bfloat16 [4, 4096, 960], P('dp', 'seq'), may hold values from -6 to 6
Outputs:
- block_output: bfloat16 [4, 4096, 960], P('dp', 'seq')
- input_gradient: float32 [4, 4096, 960], P('dp', 'seq')
- project_gradient: float32 [2, 960, 1600], P(None, 'dp', 'seq')
- output_gradient: float32 [2, 960, 960], P(None, 'dp', 'seq')
- expand_gradient: float32 [2, 960, 5120], P(None, 'dp', 'seq')
- contract_gradient: float32 [2, 2560, 960], P(None, 'dp', 'seq')
- gains_gradient: float32 [3840], P(('dp', 'seq'))
The draws below stay inside these ranges and needn't reach their ends.
Inputs may be any that keep to these rules, and one draw needn't show every extreme that they name: `segments`: in each sequence the documents are numbered 0, 1, 2, ... in order of position, none empty. In one sequence of each draw, document 0 ends within the first 128 positions, document 1 runs to within the last 128 positions and document 2 fills the rest. In the sequence after it (cyclically) every document has max(200, 2) positions, except the last, which is cut at the sequence's end. In every other sequence the documents have max(200, 2) to 2000 positions each, except the last, which is cut at the sequence's end.
All inputs are finite; a program needn't handle non-finite values.
Results may differ from the reference program's by a relative error of at most 0.03.
Values may be sent and summed in bfloat16 or wider, within the bound.
No kernel may reach another device: no remote copies, remote signals or barrier semaphores. Data moves between devices by JAX's collectives and lax.ppermute only.
A program may use at most 192 MiB of HBM per device.

```python
import math
import jax
import jax.numpy as jnp
from jax import lax

D = 960
HEADS = 15
KV_HEADS = 5
HEAD = 64
FF = 2560
LAYERS = 2
TOK_DEV = 128
LENGTH = 4096
SEQS = 4
KVD = 320


def draw_segments(key, part):
    key = jax.random.fold_in(key, 11)
    first_key, last_key, length_key, pick_key = jax.random.split(key, 4)
    index = jnp.arange(LENGTH, dtype=jnp.int32)
    shortest = max(LENGTH * 200 // 4096, 2)
    longest = max(LENGTH * 2000 // 4096, shortest + 1)
    count = LENGTH // shortest + 1
    head_length = jax.random.randint(first_key, (SEQS, 1), 1, TOK_DEV)
    tail_length = jax.random.randint(last_key, (SEQS, 1), 1, TOK_DEV)
    spanning = (index[None, :] >= head_length).astype(jnp.int32) + (index[None, :] >= LENGTH - tail_length).astype(jnp.int32)
    doc_lengths = jax.random.randint(length_key, (SEQS, count), shortest, longest + 1)
    ends = jnp.cumsum(doc_lengths, axis=1)
    packed = jnp.sum((ends[:, None, :] <= index[None, :, None]).astype(jnp.int32), axis=2)
    densest = jnp.broadcast_to((index // shortest)[None, :], (SEQS, LENGTH))
    chosen = jax.random.randint(pick_key, (), 0, SEQS)
    follower = (chosen + 1) % SEQS
    rows = jnp.arange(SEQS, dtype=jnp.int32)[:, None]
    result = jnp.where(rows == follower, densest, packed)
    return jnp.where(rows == chosen, spanning, result).astype(jnp.int32)


def shard_levels(key, shape, cuts, low, largest):
    factor_of = 1.0
    for axis_at, blocks in cuts:
        heights = jax.random.uniform(jax.random.fold_in(jax.random.fold_in(key, 6), axis_at), (blocks,), jnp.float32, low / len(cuts), largest / len(cuts))
        factor_of = factor_of * jnp.repeat(jnp.exp(heights), shape[axis_at] // blocks).reshape((-1,) + (1,) * (len(shape) - 1 - axis_at))
    return factor_of


def centred(rng, dims, deviation, reach, cuts=(), held_as=jnp.bfloat16):
    values = deviation * jax.random.normal(rng, dims, jnp.float32)
    if cuts:
        values = values * shard_levels(rng, dims, cuts, -0.22, 0.18)
    return jnp.clip(values, -reach, reach).astype(held_as)


def setup_inputs(seed: int = 0) -> dict:
    key_list = jax.random.split(jax.random.key(seed), 9)
    inputs = centred(key_list[0], (SEQS, LENGTH, D), 1.0, 6.0, ((0, 4), (1, 32)))
    w_project = centred(key_list[1], (LAYERS, D, D + 2 * KVD), D ** -0.5, 0.1875, ((1, 4), (2, 32)))
    w_output = centred(key_list[2], (LAYERS, D, D), (max(D // 64, 2)) ** -0.5, 1.5, ((1, 4), (2, 32)))
    w_expand = centred(key_list[3], (LAYERS, D, 2 * FF), D ** -0.5, 0.1875, ((1, 4), (2, 32)))
    w_contract = centred(key_list[4], (LAYERS, FF, D), FF ** -0.5, 0.125, ((1, 4), (2, 32)))
    norm_gains = jnp.clip(1.0 + 0.1 * jax.random.normal(key_list[5], (2 * LAYERS * D,), jnp.float32), 0.5, 1.5).astype(jnp.bfloat16)
    segments = draw_segments(jax.random.fold_in(key_list[8], 71), 0)
    cotangent = centred(key_list[7], (SEQS, LENGTH, D), 1.0, 6.0, ((0, 4), (1, 32)))
    return {"inputs": inputs, "w_project": w_project, "w_output": w_output, "w_expand": w_expand, "w_contract": w_contract, "norm_gains": norm_gains, "segments": segments, "cotangent": cotangent}


EPSILON = 1e-05
THETA = 100000.0
MASKED = -1e+30
HIGHEST = lax.Precision.HIGHEST

@jax.custom_vjp
def low(v):
    return lax.optimization_barrier(v.astype(jnp.bfloat16)).astype(jnp.float32)

@jax.custom_vjp
def low_back(v):
    return v

def low_keep(v):
    return (low(v), None)

def low_pass(kept, grad):
    return (grad,)

def back_keep(v):
    return (v, None)

def back_low(kept, grad):
    return (low(grad),)
low.defvjp(low_keep, low_pass)
low_back.defvjp(back_keep, back_low)

def frequencies(size):
    half = size // 2
    return 1.0 / THETA ** (jnp.arange(half, dtype=jnp.float32) * 2.0 / size)

def rotate(values, cosine, sine):
    half = values.shape[-1] // 2
    first = values[..., :half]
    second = values[..., half:]
    return jnp.concatenate([first * cosine - second * sine, second * cosine + first * sine], axis=-1)

def root_norm(stream, gain):
    scale = lax.rsqrt(lax.optimization_barrier(jnp.mean(stream * stream, axis=-1, keepdims=True)) + EPSILON)
    return stream * scale * gain

def gated_unit(gate_up):
    width = gate_up.shape[-1] // 2
    gate = gate_up[..., :width]
    return gate / (1.0 + jnp.exp(-gate)) * gate_up[..., width:]

def product(left, right):
    return jnp.dot(left, right, precision=HIGHEST)

def attend(queries, keys, values, segment, scale):
    length = queries.shape[0]
    block = 512 if length % 512 == 0 else length
    count = length // block
    index = jnp.arange(length, dtype=jnp.int32)
    grouped = queries.reshape(count, block, KV_HEADS, HEADS // KV_HEADS, HEAD)

    def one_block(pieces):
        query_block, segment_block, index_block = pieces
        scores = low_back(jnp.einsum('qkgd,tkd->kgqt', query_block, keys, precision=HIGHEST) * scale)
        allowed = (segment_block[:, None] == segment[None, :]) & (index_block[:, None] >= index[None, :])
        scores = jnp.where(allowed[None, None], scores, MASKED)
        top = lax.optimization_barrier(jnp.max(scores, axis=-1, keepdims=True))
        raised = jnp.exp(scores - top)
        chance = raised / lax.optimization_barrier(jnp.sum(raised, axis=-1, keepdims=True))
        mixed = jnp.einsum('kgqt,tkd->qkgd', low(chance), values, precision=HIGHEST)
        return mixed.reshape(block, HEADS * HEAD)
    result = lax.map(jax.checkpoint(one_block), (grouped, segment.reshape(count, block), index.reshape(count, block)))
    return result.reshape(length, HEADS * HEAD)

def run_sequence(stream, weights, segment, cosine, sine):
    w_project, w_output, w_expand, w_contract, gains = weights
    scale = 1.0 / math.sqrt(HEAD)
    key_width = KV_HEADS * HEAD
    for layer in range(LAYERS):
        normed = low(root_norm(stream, gains[layer, 0]))
        projected = low_back(product(normed, w_project[layer]))
        queries = low(rotate(projected[:, :D].reshape(-1, HEADS, HEAD), cosine, sine))
        keys = low(rotate(projected[:, D:D + key_width].reshape(-1, KV_HEADS, HEAD), cosine, sine))
        values = low(projected[:, D + key_width:].reshape(-1, KV_HEADS, HEAD))
        mixed = low_back(low(attend(queries, keys, values, segment, scale)))
        stream = stream + low_back(product(mixed, w_output[layer]))
        normed_feed = low(root_norm(stream, gains[layer, 1]))
        gate_up = low_back(product(normed_feed, w_expand[layer]))
        hidden = low(gated_unit(gate_up))
        stream = stream + low_back(product(hidden, w_contract[layer]))
    return stream

def reference(inputs, w_project, w_output, w_expand, w_contract, norm_gains, segments, cotangent):
    index = jnp.arange(LENGTH, dtype=jnp.int32)

    def starts_of(segment):
        return lax.optimization_barrier(jnp.sum((segment[None, :] < segment[:, None]).astype(jnp.int32), axis=1))
    starts = lax.map(starts_of, segments)
    position = (index[None, :] - starts).astype(jnp.float32)
    angle = position[:, :, None] * frequencies(HEAD)[None, None, :]
    cosine = jnp.cos(angle)[:, :, None, :]
    sine = jnp.sin(angle)[:, :, None, :]

    def forward(stream, project, output, expand, contract, gains):
        weights = (project, output, expand, contract, gains.reshape(LAYERS, 2, D))

        def one_sequence(pieces):
            return run_sequence(pieces[0], weights, pieces[1], pieces[2], pieces[3])
        return lax.map(one_sequence, (stream, segments, cosine, sine))
    result, pull = jax.vjp(forward, inputs.astype(jnp.float32), w_project.astype(jnp.float32), w_output.astype(jnp.float32), w_expand.astype(jnp.float32), w_contract.astype(jnp.float32), norm_gains.astype(jnp.float32))
    grads = pull(cotangent.astype(jnp.float32))
    return (result.astype(jnp.bfloat16), grads[0], grads[1], grads[2], grads[3], grads[4], grads[5])
```

```python
import math

import jax
import jax.numpy as jnp
from jax import lax
from jax.experimental import pallas as pl
from jax.experimental.pallas import tpu as pltpu
from jax.sharding import PartitionSpec as P

HEADS = 15
KV_HEADS = 5
HEAD = 64
GROUP = HEADS // KV_HEADS
KVD = KV_HEADS * HEAD

EPSILON = 1e-05
THETA = 100000.0
MASKED = -1e30

RING_Y = [[z * 8 + y * 2 + c for y in range(4)] for z in range(4) for c in range(2)]
RING_Z = [[z * 8 + y * 2 + c for z in range(4)] for y in range(4) for c in range(2)]
PLANE = [[i * 2 + c for i in range(16)] for c in range(2)]
SWAP = [(i, i ^ 1) for i in range(32)]

R_EXPAND = 160
R_PROJECT = 64
R_OUTPUT = 32
R_CONTRACT = 96


def frequencies(size):
    half = size // 2
    return 1.0 / THETA ** (jnp.arange(half, dtype=jnp.float32) * 2.0 / size)


def rotate(values, cosine, sine):
    half = values.shape[-1] // 2
    first = values[..., :half]
    second = values[..., half:]
    return jnp.concatenate(
        [first * cosine - second * sine, second * cosine + first * sine], axis=-1
    )


def root_norm(stream, gain):
    scale = lax.rsqrt(jnp.mean(stream * stream, axis=-1, keepdims=True) + EPSILON)
    return stream * scale * gain


def gated_unit(gate_up):
    width = gate_up.shape[-1] // 2
    gate = gate_up[..., :width]
    return gate / (1.0 + jnp.exp(-gate)) * gate_up[..., width:]


def plain_dot(left, right):
    return jnp.dot(left, right, preferred_element_type=jnp.float32)


def contract_rows(left, right):
    return lax.dot_general(
        left, right, (((0,), (0,)), ((), ())), preferred_element_type=jnp.float32
    )


def contract_cols(left, right):
    return lax.dot_general(
        left, right, (((1,), (1,)), ((), ())), preferred_element_type=jnp.float32
    )


def pad_rows(array, rows, axis):
    widths = [(0, 0)] * array.ndim
    widths[axis] = (0, rows - array.shape[axis])
    return jnp.pad(array, widths)


def swap_cores(array):
    return lax.ppermute(array, "seq", SWAP)


def gather_seq(array):
    along_y = lax.all_gather(array, "seq", axis_index_groups=RING_Y)
    plane = lax.all_gather(along_y, "seq", axis_index_groups=RING_Z)
    other = swap_cores(plane)
    core = lax.axis_index("seq") % 2
    first = jnp.where(core == 0, plane, other)
    second = jnp.where(core == 0, other, plane)
    return jnp.stack([first, second], axis=2).reshape((32,) + array.shape)


def reduce_seq(array):
    pairs = array.reshape((16, 2) + array.shape[1:])
    core = lax.axis_index("seq") % 2
    mine = jnp.where(core == 0, pairs[:, 0], pairs[:, 1])
    theirs = jnp.where(core == 0, pairs[:, 1], pairs[:, 0])
    arrived = swap_cores(theirs)
    both = (mine.astype(jnp.float32) + arrived.astype(jnp.float32)).astype(jnp.bfloat16)
    spread = lax.all_to_all(both, "seq", 0, 0, axis_index_groups=PLANE, tiled=True)
    return jnp.sum(spread.astype(jnp.float32), axis=0)


def reduce_dp(array):
    rows = array.shape[0]
    parts = array.reshape(rows, 4, 240).transpose(1, 0, 2).astype(jnp.bfloat16)
    spread = lax.all_to_all(parts, "dp", 0, 0, tiled=True)
    return jnp.sum(spread.astype(jnp.float32), axis=0)


def reduce_bulk(array):
    narrow = R_EXPAND + R_OUTPUT
    first = array[:narrow].reshape(narrow, 4, 240).transpose(1, 0, 2)
    last = array[narrow:].reshape(3, 32, 960).transpose(1, 0, 2).reshape(32, 2880)[:, :2560]
    last = last.reshape(32, 4, 640).transpose(1, 0, 2)
    last = jnp.pad(last, ((0, 0), (0, 0), (0, 80))).reshape(4, R_CONTRACT, 240)
    parts = jnp.concatenate([first, last], axis=1).astype(jnp.bfloat16)
    spread = lax.all_to_all(parts, "dp", 0, 0, tiled=True)
    return jnp.sum(spread.astype(jnp.float32), axis=0)


def gather_dp(array):
    parts = lax.all_gather(array, "dp")
    return parts.transpose(1, 0, 2).reshape(array.shape[0], 4 * array.shape[1])


def pack_contract(rows):
    wide = jnp.pad(rows, ((0, 0), (0, 320)))
    return wide.reshape(32, 3, 960).transpose(1, 0, 2).reshape(R_CONTRACT, 960)


def unpack_contract(block):
    wide = block.reshape(32, 3, 32, 960).transpose(0, 2, 1, 3).reshape(32, 32, 2880)
    return wide[:, :30, :2560].reshape(960, 2560)


def spread_contract(grad):
    wide = jnp.pad(grad.reshape(32, 30, 2560), ((0, 0), (0, 2), (0, 320)))
    return wide.reshape(32, 32, 3, 960).transpose(0, 2, 1, 3).reshape(32, R_CONTRACT, 960)


CHUNK = 512


def nt_dot(left, right):
    return lax.dot_general(
        left, right, (((1,), (1,)), ((), ())), preferred_element_type=jnp.float32
    )


def tn_dot(left, right):
    return lax.dot_general(
        left, right, (((0,), (0,)), ((), ())), preferred_element_type=jnp.float32
    )


def take_heads(ref, head):
    return jnp.concatenate(
        [ref[:, (GROUP * head + g) * HEAD : (GROUP * head + g + 1) * HEAD] for g in range(GROUP)],
        axis=0,
    )


def take_row(ref, head):
    return jnp.concatenate(
        [ref[GROUP * head + g : GROUP * head + g + 1, :] for g in range(GROUP)], axis=1
    )


def forward_kernel(range_ref, query_ref, packed_ref, bias_ref, mixed_ref, total_ref):
    tok_rows = query_ref.shape[0]
    lanes = GROUP * tok_rows
    low, high = range_ref[0], range_ref[1]
    for head in range(KV_HEADS):
        query = take_heads(query_ref, head)

        def step(index, carry, head=head, query=query):
            top, total, mixed = carry
            rows = pl.ds(pl.multiple_of(index * CHUNK, CHUNK), CHUNK)
            key = packed_ref[rows, head * HEAD : (head + 1) * HEAD]
            value = packed_ref[rows, KVD + head * HEAD : KVD + (head + 1) * HEAD]
            bias = bias_ref[rows, :]
            scores = nt_dot(key, query) + jnp.concatenate([bias] * GROUP, axis=1)
            new_top = jnp.maximum(top, jnp.max(scores, axis=0, keepdims=True))
            raised = jnp.exp(scores - new_top)
            shrink = jnp.exp(top - new_top)
            total = total * shrink + jnp.sum(raised, axis=0, keepdims=True)
            mixed = mixed * shrink + tn_dot(value, raised.astype(jnp.bfloat16))
            return new_top, total, mixed

        start = (
            jnp.full((1, lanes), MASKED, jnp.float32),
            jnp.zeros((1, lanes), jnp.float32),
            jnp.zeros((HEAD, lanes), jnp.float32),
        )
        top, total, mixed = lax.fori_loop(low, high, step, start)
        mixed = mixed / total
        log_total = top + jnp.log(total)
        for g in range(GROUP):
            at = GROUP * head + g
            columns = slice(g * tok_rows, (g + 1) * tok_rows)
            mixed_ref[at * HEAD : (at + 1) * HEAD, :] = mixed[:, columns]
            total_ref[at : at + 1, :] = log_total[:, columns]


def backward_kernel(
    range_ref, query_ref, packed_ref, bias_ref, total_ref, inner_ref, grad_ref, query_out, packed_out
):
    tok_rows = query_ref.shape[0]
    low, high = range_ref[0], range_ref[1]
    packed_out[...] = jnp.zeros(packed_out.shape, packed_out.dtype)
    for head in range(KV_HEADS):
        query = take_heads(query_ref, head)
        grad = take_heads(grad_ref, head)
        log_total = take_row(total_ref, head)
        inner = take_row(inner_ref, head)
        key_lanes = slice(head * HEAD, (head + 1) * HEAD)
        value_lanes = slice(KVD + head * HEAD, KVD + (head + 1) * HEAD)

        def step(
            index,
            total,
            query=query,
            grad=grad,
            log_total=log_total,
            inner=inner,
            key_lanes=key_lanes,
            value_lanes=value_lanes,
        ):
            rows = pl.ds(pl.multiple_of(index * CHUNK, CHUNK), CHUNK)
            key = packed_ref[rows, key_lanes]
            value = packed_ref[rows, value_lanes]
            bias = bias_ref[rows, :]
            scores = nt_dot(key, query) + jnp.concatenate([bias] * GROUP, axis=1)
            chance = jnp.exp(scores - log_total)
            grad_chance = nt_dot(value, grad)
            grad_scores = (chance * (grad_chance - inner)).astype(jnp.bfloat16)
            packed_out[rows, key_lanes] = plain_dot(grad_scores, query).astype(jnp.bfloat16)
            packed_out[rows, value_lanes] = plain_dot(
                chance.astype(jnp.bfloat16), grad
            ).astype(jnp.bfloat16)
            return total + tn_dot(key, grad_scores)

        start = jnp.zeros((HEAD, GROUP * tok_rows), jnp.float32)
        grad_query = lax.fori_loop(low, high, step, start) * (1.0 / math.sqrt(HEAD))
        for g in range(GROUP):
            at = GROUP * head + g
            query_out[at * HEAD : (at + 1) * HEAD, :] = grad_query[
                :, g * tok_rows : (g + 1) * tok_rows
            ]


IN_VMEM = pl.BlockSpec(memory_space=pltpu.VMEM)
IN_SMEM = pl.BlockSpec(memory_space=pltpu.SMEM)


def attend_forward(queries, packed, bias, chunk_range):
    tok_rows = queries.shape[0]
    return pl.pallas_call(
        forward_kernel,
        out_shape=(
            jax.ShapeDtypeStruct((HEADS * HEAD, tok_rows), jnp.float32),
            jax.ShapeDtypeStruct((HEADS, tok_rows), jnp.float32),
        ),
        in_specs=[IN_SMEM, IN_VMEM, IN_VMEM, IN_VMEM],
        out_specs=(IN_VMEM, IN_VMEM),
        compiler_params=pltpu.CompilerParams(vmem_limit_bytes=40 << 20),
        cost_estimate=pl.CostEstimate(
            flops=4 * 4096 * 128 * 960, bytes_accessed=8 << 20, transcendentals=4096 * 128 * 15
        ),
    )(chunk_range, queries, packed, bias)


def attend_backward(queries, packed, bias, chunk_range, log_total, inner, grad_mixed):
    tok_rows = queries.shape[0]
    return pl.pallas_call(
        backward_kernel,
        out_shape=(
            jax.ShapeDtypeStruct((HEADS * HEAD, tok_rows), jnp.float32),
            jax.ShapeDtypeStruct(packed.shape, jnp.bfloat16),
        ),
        in_specs=[IN_SMEM] + [IN_VMEM] * 6,
        out_specs=(IN_VMEM, IN_VMEM),
        compiler_params=pltpu.CompilerParams(vmem_limit_bytes=40 << 20),
        cost_estimate=pl.CostEstimate(
            flops=10 * 4096 * 128 * 960, bytes_accessed=13 << 20, transcendentals=4096 * 128 * 15
        ),
    )(chunk_range, queries, packed, bias, log_total, inner, grad_mixed)


def norm_backward(stream, gain, grad):
    return jax.vjp(root_norm, stream, gain)[1](grad)


def on_device(inputs, w_project, w_output, w_expand, w_contract, norm_gains, segments, cotangent):
    tok_rows = inputs.shape[1]
    width = inputs.shape[2]
    layers = w_project.shape[0]
    local_segment = segments[0]

    gain_row = jnp.pad(norm_gains[None, :], ((0, 0), (0, 240 - 30)))
    lead = jnp.concatenate([w_project[0].T, gain_row], axis=0)
    lead = gather_dp(pad_rows(lead, R_PROJECT, 0))
    segment_row = jnp.pad(
        local_segment.astype(jnp.bfloat16)[None, :], ((0, 0), (0, width - tok_rows))
    )
    lead = jnp.concatenate([lead[:51], segment_row, lead[52:]], axis=0)

    narrow = [w_expand[0].T, pad_rows(w_output[0].T, R_OUTPUT, 0)]
    narrow += [w_expand[1].T, pad_rows(w_output[1].T, R_OUTPUT, 0)]
    narrow += [pad_rows(w_project[1].T, R_PROJECT, 0)]
    narrow = gather_dp(jnp.concatenate(narrow, axis=0))
    wide = gather_dp(
        pad_rows(w_contract.transpose(0, 2, 1), R_OUTPUT, 1).reshape(2 * R_OUTPUT, 640)
    )
    bulk = jnp.concatenate(
        [narrow, pack_contract(wide[:R_OUTPUT]), pack_contract(wide[R_OUTPUT:])], axis=0
    )
    bulk = lax.all_gather(bulk, "seq")

    def take(start, rows, used):
        return bulk[:, start : start + rows][:, :used].reshape(32 * used, width)

    leads = gather_seq(lead)
    gains = (
        leads[:, 50, :].reshape(32, 4, 240)[:, :, :30].transpose(1, 0, 2).reshape(-1)
    ).astype(jnp.float32)
    all_segment = leads[:, 51, :tok_rows].reshape(-1).astype(jnp.int32)
    length = all_segment.shape[0]
    weights = [
        (
            leads[:, :50].reshape(1600, width),
            take(160, R_OUTPUT, 30),
            take(0, R_EXPAND, R_EXPAND),
            unpack_contract(bulk[:, 448:544]),
        ),
        (
            take(384, R_PROJECT, 50),
            take(352, R_OUTPUT, 30),
            take(192, R_EXPAND, R_EXPAND),
            unpack_contract(bulk[:, 544:640]),
        ),
    ]

    query_index = lax.axis_index("seq") * tok_rows + jnp.arange(tok_rows, dtype=jnp.int32)
    key_index = jnp.arange(length, dtype=jnp.int32)
    starts = jnp.sum((all_segment[None, :] < local_segment[:, None]).astype(jnp.int32), axis=1)
    position = (query_index - starts).astype(jnp.float32)
    angle = position[:, None] * frequencies(HEAD)[None, :]
    cosine = jnp.cos(angle)[:, None, :]
    sine = jnp.sin(angle)[:, None, :]
    allowed = (local_segment[None, :] == all_segment[:, None]) & (
        query_index[None, :] >= key_index[:, None]
    )
    bias = jnp.where(allowed, 0.0, MASKED).astype(jnp.float32)
    chunk_range = jnp.stack([starts[0] // CHUNK, query_index[-1] // CHUNK + 1])
    scale = 1.0 / math.sqrt(HEAD)
    stream = inputs[0].astype(jnp.float32)
    records = []
    for layer in range(layers):
        project, output, expand, contract = weights[layer]
        gain_attend = gains[2 * layer * width : (2 * layer + 1) * width]
        gain_feed = gains[(2 * layer + 1) * width : (2 * layer + 2) * width]
        normed = root_norm(stream, gain_attend).astype(jnp.bfloat16)
        projected = contract_cols(normed, project)
        queries = (
            (rotate(projected[:, :width].reshape(tok_rows, HEADS, HEAD), cosine, sine) * scale)
            .astype(jnp.bfloat16)
            .reshape(tok_rows, width)
        )
        keys = rotate(
            projected[:, width : width + KVD].reshape(tok_rows, KV_HEADS, HEAD), cosine, sine
        ).astype(jnp.bfloat16)
        values = projected[:, width + KVD :].astype(jnp.bfloat16)
        packed = gather_seq(
            jnp.concatenate([keys.reshape(tok_rows, KVD), values], axis=1)
        ).reshape(length, 2 * KVD)
        mixed_wide, log_total = attend_forward(queries, packed, bias, chunk_range)
        mixed_wide = mixed_wide.T
        mixed = mixed_wide.astype(jnp.bfloat16)
        middle = stream + contract_cols(mixed, output)
        normed_feed = root_norm(middle, gain_feed).astype(jnp.bfloat16)
        gate_up = contract_cols(normed_feed, expand)
        hidden = gated_unit(gate_up).astype(jnp.bfloat16)
        records.append(
            (
                stream,
                normed,
                queries,
                packed,
                log_total,
                mixed_wide,
                mixed,
                middle,
                normed_feed,
                gate_up,
                hidden,
            )
        )
        stream = middle + contract_cols(hidden, contract)
    block_output = stream.astype(jnp.bfloat16)[None]

    grad_stream = cotangent[0].astype(jnp.float32)
    bulk_grads = [None] * layers
    project_grads = [None] * layers
    gain_grads = [None] * layers
    for layer in reversed(range(layers)):
        project, output, expand, contract = weights[layer]
        (
            stream_in,
            normed,
            queries,
            packed,
            log_total,
            mixed_wide,
            mixed,
            middle,
            normed_feed,
            gate_up,
            hidden,
        ) = records[layer]
        gain_attend = gains[2 * layer * width : (2 * layer + 1) * width]
        gain_feed = gains[(2 * layer + 1) * width : (2 * layer + 2) * width]
        grad_low = grad_stream.astype(jnp.bfloat16)
        grad_contract = contract_rows(grad_low, hidden).astype(jnp.bfloat16)
        grad_hidden = plain_dot(grad_low, contract)
        grad_gate_up = jax.vjp(gated_unit, gate_up)[1](grad_hidden)[0].astype(jnp.bfloat16)
        grad_expand = contract_rows(grad_gate_up, normed_feed).astype(jnp.bfloat16)
        grad_feed = plain_dot(grad_gate_up, expand)
        grad_middle_part, grad_gain_feed = norm_backward(middle, gain_feed, grad_feed)
        grad_middle = grad_stream + grad_middle_part
        grad_middle_low = grad_middle.astype(jnp.bfloat16)
        grad_output = contract_rows(grad_middle_low, mixed).astype(jnp.bfloat16)
        bulk_grad = jnp.concatenate(
            [
                grad_expand.reshape(32, R_EXPAND, width),
                pad_rows(grad_output.reshape(32, 30, width), R_OUTPUT, 1),
                spread_contract(grad_contract),
            ],
            axis=1,
        )
        bulk_grads[layer] = lax.psum_scatter(bulk_grad, "seq", scatter_dimension=0)
        grad_mixed = plain_dot(grad_middle_low, output).astype(jnp.bfloat16)
        inner = jnp.sum(
            (grad_mixed.astype(jnp.float32) * mixed_wide).reshape(tok_rows, HEADS, HEAD), axis=2
        ).T
        grad_query, grad_packed = attend_backward(
            queries, packed, bias, chunk_range, log_total, inner, grad_mixed
        )
        grad_query = grad_query.T
        grad_local = reduce_seq(grad_packed.reshape(32, tok_rows, 2 * KVD))
        grad_query = rotate(grad_query.reshape(tok_rows, HEADS, HEAD), cosine, -sine)
        grad_key = rotate(grad_local[:, :KVD].reshape(tok_rows, KV_HEADS, HEAD), cosine, -sine)
        grad_projected = jnp.concatenate(
            [
                grad_query.reshape(tok_rows, width),
                grad_key.reshape(tok_rows, KVD),
                grad_local[:, KVD:],
            ],
            axis=1,
        ).astype(jnp.bfloat16)
        grad_project = contract_rows(grad_projected, normed).astype(jnp.bfloat16)
        grad_normed = plain_dot(grad_projected, project)
        grad_input_part, grad_gain_attend = norm_backward(stream_in, gain_attend, grad_normed)
        grad_stream = grad_middle + grad_input_part
        gain_grads[layer] = jnp.concatenate([grad_gain_attend, grad_gain_feed])
        project_rows = grad_project.reshape(32, 50, width)
        if layer == 0:
            gain_rows = (
                jnp.concatenate(gain_grads)
                .reshape(4, 32, 30)
                .transpose(1, 0, 2)
                .astype(jnp.bfloat16)
            )
            gain_rows = pad_rows(gain_rows, 240, 2).reshape(32, 1, width)
            project_rows = jnp.concatenate([project_rows, gain_rows], axis=1)
        project_rows = pad_rows(project_rows, R_PROJECT, 1)
        project_grads[layer] = reduce_dp(reduce_seq(project_rows))

    parts = [reduce_bulk(grad) for grad in bulk_grads]
    expand_out = jnp.stack([part[:R_EXPAND].T for part in parts])
    output_out = jnp.stack([part[R_EXPAND : R_EXPAND + 30].T for part in parts])
    contract_out = jnp.stack(
        [part[R_EXPAND + R_OUTPUT :].reshape(32, 720)[:30, :640].T for part in parts]
    )
    project_out = jnp.stack([part[:50].T for part in project_grads])
    gains_out = project_grads[0][50, :30]
    return (
        block_output,
        grad_stream[None],
        project_out,
        output_out,
        expand_out,
        contract_out,
        gains_out,
    )


def solution(mesh):
    in_specs = (
        P("dp", "seq", None),
        P(None, "dp", "seq"),
        P(None, "dp", "seq"),
        P(None, "dp", "seq"),
        P(None, "dp", "seq"),
        P(("dp", "seq")),
        P("dp", "seq"),
        P("dp", "seq", None),
    )
    out_specs = (
        P("dp", "seq", None),
        P("dp", "seq", None),
        P(None, "dp", "seq"),
        P(None, "dp", "seq"),
        P(None, "dp", "seq"),
        P(None, "dp", "seq"),
        P(("dp", "seq")),
    )
    return jax.shard_map(
        on_device, mesh=mesh, in_specs=in_specs, out_specs=out_specs, check_vma=False
    )
```

```python
import functools
import math

import jax
import jax.numpy as jnp
from jax import lax
from jax.experimental import pallas as pl
from jax.experimental.pallas import tpu as pltpu
from jax.sharding import PartitionSpec as P

HEADS = 15
KV_HEADS = 5
HEAD = 64
GROUP = HEADS // KV_HEADS
KVD = KV_HEADS * HEAD
WIDTH = 960
FF = 2560

EPSILON = 1e-05
THETA = 100000.0
MASKED = -1e30

RING_Y = [[z * 8 + y * 2 + c for y in range(4)] for z in range(4) for c in range(2)]
PLANE = [[i * 2 + c for i in range(16)] for c in range(2)]
SWAP = [(i, i ^ 1) for i in range(32)]

PADDED = 1024
EXPAND = 320
CONTRACT = 160
OUTPUT = 64
PROJECT = 128
LEAD = 144
GRADS = EXPAND + CONTRACT + OUTPUT
CHUNK = 512
LIMIT = 40 << 20

F32 = jnp.float32
BF16 = jnp.bfloat16
IN_VMEM = pl.BlockSpec(memory_space=pltpu.VMEM)
IN_SMEM = pl.BlockSpec(memory_space=pltpu.SMEM)


def shape(dims, dtype):
    return jax.ShapeDtypeStruct(dims, dtype)


def params():
    return pltpu.CompilerParams(vmem_limit_bytes=LIMIT)


def cost(flops, traffic):
    return pl.CostEstimate(flops=flops, bytes_accessed=traffic, transcendentals=0)


def nn_dot(left, right):
    return jnp.dot(left, right, preferred_element_type=F32)


def nt_dot(left, right):
    return lax.dot_general(left, right, (((1,), (1,)), ((), ())), preferred_element_type=F32)


def tn_dot(left, right):
    return lax.dot_general(left, right, (((0,), (0,)), ((), ())), preferred_element_type=F32)


def frequencies(size):
    half = size // 2
    return 1.0 / THETA ** (jnp.arange(half, dtype=F32) * 2.0 / size)


def norm_scale(stream):
    return lax.rsqrt(jnp.sum(stream * stream, axis=1, keepdims=True) / WIDTH + EPSILON)


def norm_pull(stream, gain, grad):
    scale = norm_scale(stream)
    weighted = gain * grad
    mean = jnp.sum(weighted * stream, axis=1, keepdims=True) / WIDTH
    grad_stream = scale * weighted - stream * (scale * scale * scale * mean)
    return grad_stream, jnp.sum(grad * stream * scale, axis=0, keepdims=True)


def tiles(ref, devices, start, rows, count, first):
    pieces = []
    for dp in range(ref.shape[0]):
        for tile in range(count):
            at = first + tile * rows
            block = ref[dp, start : start + devices, at : at + rows, :]
            pieces.append(block.reshape(devices * rows, 128))
    return jnp.concatenate(pieces, axis=1)


def project_kernel(stream_ref, gain_ref, weight_ref, cosine_ref, sine_ref, *rest):
    query_ref, packed_ref, normed_ref, natural = rest
    stream = stream_ref[...]
    normed = (stream * norm_scale(stream) * gain_ref[...]).astype(BF16)
    normed_ref[...] = normed
    for part in range(4):
        result = nt_dot(tiles(weight_ref, 8, part * 8, 64, 2, 0), normed)
        for s in range(8):
            at = part * 8 + s
            natural[at * 50 : at * 50 + 50, :] = result[s * 64 : s * 64 + 50, :]
    cosine, sine = cosine_ref[...], sine_ref[...]
    for head in range(HEADS + KV_HEADS):
        at = head * HEAD
        first = natural[at : at + 32, :]
        second = natural[at + 32 : at + 64, :]
        one = first * cosine - second * sine
        two = second * cosine + first * sine
        if head < HEADS:
            both = jnp.concatenate([one, two], axis=0) * (1.0 / math.sqrt(HEAD))
            query_ref[at : at + 64, :] = both.astype(BF16)
        else:
            natural[at : at + 32, :] = one
            natural[at + 32 : at + 64, :] = two
    packed_ref[...] = natural[WIDTH : WIDTH + 2 * KVD, :].T.astype(BF16)


def project_forward(stream, gain, weight, cosine, sine):
    tok = stream.shape[0]
    return pl.pallas_call(
        project_kernel,
        out_shape=(
            shape((WIDTH, tok), BF16),
            shape((tok, 2 * KVD), BF16),
            shape((tok, PADDED), BF16),
        ),
        in_specs=[IN_VMEM] * 5,
        out_specs=(IN_VMEM,) * 3,
        scratch_shapes=[pltpu.VMEM((WIDTH + 2 * KVD, tok), F32)],
        compiler_params=params(),
        cost_estimate=cost(2 * tok * 2048 * 1024, 5 << 20),
    )(stream, gain, weight, cosine, sine)


def take_heads(ref, head):
    return jnp.concatenate(
        [ref[(GROUP * head + g) * HEAD : (GROUP * head + g + 1) * HEAD, :] for g in range(GROUP)],
        axis=1,
    )


def take_row(ref, head):
    return jnp.concatenate(
        [ref[GROUP * head + g : GROUP * head + g + 1, :] for g in range(GROUP)], axis=1
    )


def forward_kernel(
    range_ref, query_ref, packed_ref, bias_ref, mixed_ref, total_ref, top, total, mixed
):
    tok = query_ref.shape[1]
    top[...] = jnp.full(top.shape, MASKED, F32)
    total[...] = jnp.zeros(total.shape, F32)
    mixed[...] = jnp.zeros(mixed.shape, F32)

    def step(index, carry):
        rows = pl.ds(pl.multiple_of(index * CHUNK, CHUNK), CHUNK)
        bias = jnp.concatenate([bias_ref[rows, :]] * GROUP, axis=1)

        def scores_of(head):
            key = packed_ref[rows, head * HEAD : (head + 1) * HEAD]
            return nn_dot(key, take_heads(query_ref, head)) + bias

        later = scores_of(0)
        for head in range(KV_HEADS):
            scores = later
            if head + 1 < KV_HEADS:
                later = scores_of(head + 1)
            value = packed_ref[rows, KVD + head * HEAD : KVD + (head + 1) * HEAD]
            old_top = top[head]
            new_top = jnp.maximum(old_top, jnp.max(scores, axis=0, keepdims=True))
            raised = jnp.exp(scores - new_top)
            shrink = jnp.exp(old_top - new_top)
            top[head] = new_top
            total[head] = total[head] * shrink + jnp.sum(raised, axis=0, keepdims=True)
            mixed[head] = mixed[head] * shrink + tn_dot(value, raised.astype(BF16))
        return carry

    lax.fori_loop(range_ref[0], range_ref[1], step, 0)
    for head in range(KV_HEADS):
        result = mixed[head] / total[head]
        log_total = top[head] + jnp.log(total[head])
        for g in range(GROUP):
            at = GROUP * head + g
            columns = slice(g * tok, (g + 1) * tok)
            mixed_ref[at * HEAD : (at + 1) * HEAD, :] = result[:, columns]
            total_ref[at : at + 1, :] = log_total[:, columns]


def attend_forward(queries, packed, bias, chunk_range):
    tok = queries.shape[1]
    return pl.pallas_call(
        forward_kernel,
        out_shape=(shape((WIDTH, tok), F32), shape((HEADS, tok), F32)),
        in_specs=[IN_SMEM] + [IN_VMEM] * 3,
        out_specs=(IN_VMEM, IN_VMEM),
        scratch_shapes=[
            pltpu.VMEM((KV_HEADS, 1, GROUP * tok), F32),
            pltpu.VMEM((KV_HEADS, 1, GROUP * tok), F32),
            pltpu.VMEM((KV_HEADS, HEAD, GROUP * tok), F32),
        ],
        compiler_params=params(),
        cost_estimate=cost(4 * 4096 * 128 * 960, 8 << 20),
    )(chunk_range, queries, packed, bias)


def backward_kernel(
    range_ref,
    query_ref,
    packed_ref,
    bias_ref,
    total_ref,
    inner_ref,
    grad_ref,
    query_out,
    packed_out,
    grad_query,
):
    tok = query_ref.shape[1]
    packed_out[...] = jnp.zeros(packed_out.shape, packed_out.dtype)
    grad_query[...] = jnp.zeros(grad_query.shape, F32)

    def step(index, carry):
        rows = pl.ds(pl.multiple_of(index * CHUNK, CHUNK), CHUNK)
        bias = jnp.concatenate([bias_ref[rows, :]] * GROUP, axis=1)

        def products(head):
            key = packed_ref[rows, head * HEAD : (head + 1) * HEAD]
            value = packed_ref[rows, KVD + head * HEAD : KVD + (head + 1) * HEAD]
            scores = nn_dot(key, take_heads(query_ref, head)) + bias
            return key, scores, nn_dot(value, take_heads(grad_ref, head))

        later = products(0)
        for head in range(KV_HEADS):
            key, scores, grad_chance = later
            if head + 1 < KV_HEADS:
                later = products(head + 1)
            chance = jnp.exp(scores - take_row(total_ref, head))
            grad_scores = (chance * (grad_chance - take_row(inner_ref, head))).astype(BF16)
            grad_key = nt_dot(grad_scores, take_heads(query_ref, head)).astype(BF16)
            grad_value = nt_dot(chance.astype(BF16), take_heads(grad_ref, head)).astype(BF16)
            key_lanes = slice(head * HEAD, (head + 1) * HEAD)
            value_lanes = slice(KVD + head * HEAD, KVD + (head + 1) * HEAD)
            for block in range(CHUNK // tok):
                at = index * (CHUNK // tok // 2) + block // 2
                part = slice(block * tok, (block + 1) * tok)
                packed_out[block % 2, at, :, key_lanes] = grad_key[part, :]
                packed_out[block % 2, at, :, value_lanes] = grad_value[part, :]
            grad_query[head] += tn_dot(key, grad_scores)
        return carry

    lax.fori_loop(range_ref[0], range_ref[1], step, 0)
    for head in range(KV_HEADS):
        result = grad_query[head] * (1.0 / math.sqrt(HEAD))
        for g in range(GROUP):
            at = GROUP * head + g
            query_out[at * HEAD : (at + 1) * HEAD, :] = result[:, g * tok : (g + 1) * tok]


def attend_backward(queries, packed, bias, chunk_range, log_total, inner, grad_mixed):
    tok = queries.shape[1]
    return pl.pallas_call(
        backward_kernel,
        out_shape=(shape((WIDTH, tok), F32), shape((2, 16, tok, 2 * KVD), BF16)),
        in_specs=[IN_SMEM] + [IN_VMEM] * 6,
        out_specs=(IN_VMEM, IN_VMEM),
        scratch_shapes=[pltpu.VMEM((KV_HEADS, HEAD, GROUP * tok), F32)],
        compiler_params=params(),
        cost_estimate=cost(10 * 4096 * 128 * 960, 13 << 20),
    )(chunk_range, queries, packed, bias, log_total, inner, grad_mixed)


def feed_kernel(
    stream_ref, mixed_ref, gain_ref, output_ref, gate_w, up_w, contract_w, *rest
):
    mixed_out, middle_out, normed_out, gate_out, up_out, hidden_out, stream_out = rest
    tok = stream_ref.shape[0]

    @pl.when(pl.program_id(0) == 0)
    def _():
        pieces = []
        for dp in range(4):
            pieces += [mixed_ref[dp * 240 : dp * 240 + 240, :], jnp.zeros((16, tok), F32)]
        mixed = jnp.concatenate(pieces, axis=0).T.astype(BF16)
        mixed_out[...] = mixed
        middle = stream_ref[...] + nt_dot(mixed, tiles(output_ref, 32, 0, 32, 2, 0))
        middle_out[...] = middle
        normed_out[...] = (middle * norm_scale(middle) * gain_ref[...]).astype(BF16)
        stream_out[...] = middle

    normed = normed_out[...]
    gate = nt_dot(normed, tiles(gate_w, 4, 0, 160, 2, 0))
    up = nt_dot(normed, tiles(up_w, 4, 0, 160, 2, 0))
    gate_out[...] = gate
    up_out[...] = up
    hidden = (gate / (1.0 + jnp.exp(-gate)) * up).astype(BF16)
    hidden_out[...] = hidden
    stream_out[...] += nt_dot(hidden, tiles(contract_w, 32, 0, 32, 5, 0))


def whole(dims):
    return pl.BlockSpec(dims, lambda j: (0,) * len(dims))


def weight_specs(layer):
    return [
        pl.BlockSpec((4, 32, OUTPUT, 128), lambda j: (0, 0, 15 + layer, 0)),
        pl.BlockSpec((4, 4, EXPAND, 128), lambda j: (0, j, layer, 0)),
        pl.BlockSpec((4, 4, EXPAND, 128), lambda j: (0, j + 4, layer, 0)),
        pl.BlockSpec((1, 32, CONTRACT, 128), lambda j: (j, 0, 4 + layer, 0)),
    ]


def feed_forward(stream, mixed, gain, bulk, layer):
    tok = stream.shape[0]
    column = pl.BlockSpec((tok, 640), lambda j: (0, j))
    return pl.pallas_call(
        feed_kernel,
        grid=(4,),
        out_shape=(
            shape((tok, PADDED), BF16),
            shape((tok, PADDED), F32),
            shape((tok, PADDED), BF16),
            shape((tok, FF), F32),
            shape((tok, FF), F32),
            shape((tok, FF), BF16),
            shape((tok, PADDED), F32),
        ),
        in_specs=[whole((tok, PADDED)), whole((WIDTH, tok)), whole((1, PADDED))]
        + weight_specs(layer),
        out_specs=(whole((tok, PADDED)),) * 3 + (column,) * 3 + (whole((tok, PADDED)),),
        compiler_params=params(),
        cost_estimate=cost(2 * tok * 9000 * 1024, 18 << 20),
    )(stream, mixed, gain, bulk, bulk, bulk, bulk)


def feed_pull_kernel(
    grad_ref,
    middle_ref,
    gain_ref,
    mixed_ref,
    gate_ref,
    up_ref,
    output_ref,
    gate_w,
    up_w,
    contract_w,
    *rest,
):
    low_out, gate_out, up_out, middle_out, middle_low_out, gain_out, mixed_out, inner_out, total = rest
    index = pl.program_id(0)
    tok = grad_ref.shape[0]

    @pl.when(index == 0)
    def _():
        low_out[...] = grad_ref[...].astype(BF16)
        total[...] = jnp.zeros_like(total)

    gate, up = gate_ref[...], up_ref[...]
    grad_hidden = nn_dot(low_out[...], tiles(contract_w, 32, 0, 32, 5, 0))
    chance = 1.0 / (1.0 + jnp.exp(-gate))
    swish = gate * chance
    grad_gate = (grad_hidden * up * (chance + swish * (1.0 - chance))).astype(BF16)
    grad_up = (grad_hidden * swish).astype(BF16)
    gate_out[...] = grad_gate
    up_out[...] = grad_up
    total[...] += nn_dot(grad_gate, tiles(gate_w, 4, 0, 160, 2, 0)) + nn_dot(
        grad_up, tiles(up_w, 4, 0, 160, 2, 0)
    )

    @pl.when(index == pl.num_programs(0) - 1)
    def _():
        grad_part, grad_gain = norm_pull(middle_ref[...], gain_ref[...], total[...])
        grad_middle = grad_ref[...] + grad_part
        middle_out[...] = grad_middle
        gain_out[...] = grad_gain
        low = grad_middle.astype(BF16)
        middle_low_out[...] = low
        back = nn_dot(low, tiles(output_ref, 32, 0, 32, 2, 0)).astype(BF16).astype(F32).T
        for dp in range(4):
            mixed_out[dp * 240 : dp * 240 + 240, :] = back[dp * 256 : dp * 256 + 240, :].astype(BF16)
        for head in range(HEADS):
            rows = slice(head * HEAD, head * HEAD + HEAD)
            product = mixed_out[rows, :].astype(F32) * mixed_ref[rows, :]
            inner_out[head : head + 1, :] = jnp.sum(product, axis=0, keepdims=True)


def feed_backward(grad, middle, gain, mixed, gate, up, bulk, layer):
    tok = grad.shape[0]
    column = pl.BlockSpec((tok, 640), lambda j: (0, j))
    return pl.pallas_call(
        feed_pull_kernel,
        grid=(4,),
        out_shape=(
            shape((tok, PADDED), BF16),
            shape((tok, FF), BF16),
            shape((tok, FF), BF16),
            shape((tok, PADDED), F32),
            shape((tok, PADDED), BF16),
            shape((1, PADDED), F32),
            shape((WIDTH, tok), BF16),
            shape((HEADS, tok), F32),
        ),
        in_specs=[
            whole((tok, PADDED)),
            whole((tok, PADDED)),
            whole((1, PADDED)),
            whole((WIDTH, tok)),
            column,
            column,
        ]
        + weight_specs(layer),
        out_specs=(
            whole((tok, PADDED)),
            column,
            column,
            whole((tok, PADDED)),
            whole((tok, PADDED)),
            whole((1, PADDED)),
            whole((WIDTH, tok)),
            whole((HEADS, tok)),
        ),
        scratch_shapes=[pltpu.VMEM((tok, PADDED), F32)],
        compiler_params=params(),
        cost_estimate=cost(2 * tok * 9000 * 1024, 18 << 20),
    )(grad, middle, gain, mixed, gate, up, bulk, bulk, bulk, bulk)


def put_tiles(out_ref, result, rows, count, first):
    for dp in range(4):
        for tile in range(count):
            at = (dp * count + tile) * 128
            block = result[:, at : at + 128].reshape(4, rows, 128).astype(BF16)
            out_ref[:, dp, first + tile * rows : first + (tile + 1) * rows, :] = block


def weight_kernel(with_project, *refs):
    gate_ref, normed_ref, low_ref, hidden_ref, middle_ref, mixed_ref = refs[:6]
    out_ref = refs[-1]
    put_tiles(out_ref, tn_dot(gate_ref[0], normed_ref[...]), 160, 2, 0)
    put_tiles(out_ref, tn_dot(low_ref[...], hidden_ref[...]), 32, 5, EXPAND)
    put_tiles(out_ref, tn_dot(middle_ref[...], mixed_ref[...]), 32, 2, EXPAND + CONTRACT)
    if with_project:
        put_tiles(out_ref, nn_dot(refs[6][...], refs[7][...]), 64, 2, GRADS)


def weight_gradients(grad_gate, grad_up, normed_feed, grad_low, hidden, middle_low, mixed, project):
    tok = normed_feed.shape[0]
    rows = GRADS + (PROJECT if project else 0)
    grad_gate_up = jnp.stack([grad_gate, grad_up])
    operands = [grad_gate_up, normed_feed, grad_low, hidden, middle_low, mixed]
    in_specs = [
        pl.BlockSpec((1, tok, 640), lambda j: (j // 4, 0, j % 4)),
        whole((tok, PADDED)),
        pl.BlockSpec((tok, 128), lambda j: (0, j)),
        whole((tok, FF)),
        pl.BlockSpec((tok, 128), lambda j: (0, j)),
        whole((tok, PADDED)),
    ]
    if project:
        operands += list(project)
        in_specs += [pl.BlockSpec((256, tok), lambda j: (j, 0)), whole((tok, PADDED))]
    return pl.pallas_call(
        functools.partial(weight_kernel, bool(project)),
        grid=(8,),
        out_shape=shape((32, 4, rows, 128), BF16),
        in_specs=in_specs,
        out_specs=pl.BlockSpec((4, 4, rows, 128), lambda j: (j, 0, 0, 0)),
        compiler_params=params(),
        cost_estimate=cost(2 * tok * 11000 * 1024, 20 << 20),
    )(*operands)


def project_pull_kernel(
    query_ref, local_ref, cosine_ref, sine_ref, weight_ref, stream_ref, gain_ref, grad_ref, *rest
):
    padded_out, grad_out, gain_out, natural, spread = rest
    tok = stream_ref.shape[0]
    natural[0:WIDTH, :] = query_ref[...]
    natural[WIDTH : WIDTH + 2 * KVD, :] = local_ref[...].T
    cosine, sine = cosine_ref[...], sine_ref[...]
    for head in range(HEADS + KV_HEADS):
        at = head * HEAD
        first = natural[at : at + 32, :]
        second = natural[at + 32 : at + 64, :]
        natural[at : at + 32, :] = first * cosine + second * sine
        natural[at + 32 : at + 64, :] = second * cosine - first * sine
    for s in range(32):
        spread[s * 64 : s * 64 + 50, :] = natural[s * 50 : s * 50 + 50, :]
        spread[s * 64 + 50 : s * 64 + 64, :] = jnp.zeros((14, tok), F32)
    total = jnp.zeros((tok, PADDED), F32)
    for part in range(4):
        block = spread[part * 512 : (part + 1) * 512, :].astype(BF16)
        padded_out[part * 512 : (part + 1) * 512, :] = block
        total = total + tn_dot(block, tiles(weight_ref, 8, part * 8, 64, 2, 0))
    grad_part, grad_gain = norm_pull(stream_ref[...], gain_ref[...], total)
    grad_out[...] = grad_ref[...] + grad_part
    gain_out[...] = grad_gain


def project_backward(grad_query, grad_local, cosine, sine, weight, stream, gain, grad_middle):
    tok = stream.shape[0]
    return pl.pallas_call(
        project_pull_kernel,
        out_shape=(
            shape((2048, tok), BF16),
            shape((tok, PADDED), F32),
            shape((1, PADDED), F32),
        ),
        in_specs=[IN_VMEM] * 8,
        out_specs=(IN_VMEM,) * 3,
        scratch_shapes=[
            pltpu.VMEM((WIDTH + 2 * KVD, tok), F32),
            pltpu.VMEM((2048, tok), F32),
        ],
        compiler_params=params(),
        cost_estimate=cost(2 * tok * 2048 * 1024, 6 << 20),
    )(grad_query, grad_local, cosine, sine, weight, stream, gain, grad_middle)


def lead_kernel(padded_ref, normed_ref, gains_ref, out_ref):
    result = nn_dot(padded_ref[...], normed_ref[...])
    for dp in range(4):
        for tile in range(2):
            at = (dp * 2 + tile) * 128
            block = result[:, at : at + 128].reshape(2, 2, 64, 128).astype(BF16)
            for core in range(2):
                out_ref[core, :, dp, tile * 64 : tile * 64 + 64, :] = block[:, core]
    for core in range(2):
        for place in range(2):
            out_ref[core, place, :, PROJECT:LEAD, :] = gains_ref[place * 2 + core]


def lead_gradients(padded, normed, gains):
    tok = normed.shape[0]
    return pl.pallas_call(
        lead_kernel,
        grid=(8,),
        out_shape=shape((2, 16, 4, LEAD, 128), BF16),
        in_specs=[
            pl.BlockSpec((256, tok), lambda j: (j, 0)),
            whole((tok, PADDED)),
            pl.BlockSpec((4, 4, LEAD - PROJECT, 128), lambda j: (j, 0, 0, 0)),
        ],
        out_specs=pl.BlockSpec((2, 2, 4, LEAD, 128), lambda j: (0, j, 0, 0, 0)),
        compiler_params=params(),
        cost_estimate=cost(2 * tok * 2048 * 1024, 6 << 20),
    )(padded, normed, gains)


def swap_cores(array):
    return lax.ppermute(array, "seq", SWAP)


def hop_y(array, hop):
    moves = [(i, i // 8 * 8 + (i % 8 + 2 * hop) % 8) for i in range(32)]
    return lax.ppermute(array, "seq", moves)


def hop_z(array, hop):
    return lax.ppermute(array, "seq", [(i, (i + 8 * hop) % 32) for i in range(32)])


def ring(array, move):
    return jnp.stack([array] + [move(array, hop) for hop in (1, 2, 3)])


def order_kernel(place_ref, first_own, last_own, first_other, last_other, out_ref):
    for s in range(32):
        back_z = lax.rem(place_ref[0] - s // 8 + 4, 4)
        back_y = lax.rem(place_ref[1] - s // 2 % 4 + 4, 4)
        same = place_ref[2] == s % 2

        @pl.when(same)
        def _(s=s, back_z=back_z, back_y=back_y):
            out_ref[s, 0] = first_own[back_z, back_y]
            out_ref[s, 1] = last_own[back_y, back_z]

        @pl.when(jnp.logical_not(same))
        def _(s=s, back_z=back_z, back_y=back_y):
            out_ref[s, 0] = first_other[back_z, back_y]
            out_ref[s, 1] = last_other[back_y, back_z]


def gather_seq(array):
    index = lax.axis_index("seq")
    first = ring(array[0], hop_y)
    last = ring(array[1], hop_z)
    first = ring(first, hop_z)
    last = ring(last, hop_y)
    place = jnp.stack([index // 8, index // 2 % 4, index % 2]).astype(jnp.int32)
    return pl.pallas_call(
        order_kernel,
        out_shape=shape((32,) + array.shape, array.dtype),
        in_specs=[IN_SMEM] + [IN_VMEM] * 4,
        out_specs=IN_VMEM,
        compiler_params=params(),
        cost_estimate=cost(0, 12 << 20),
    )(place, first, last, swap_cores(first), swap_cores(last))


def reduce_seq(array):
    core = lax.axis_index("seq") % 2
    mine = lax.dynamic_index_in_dim(array, core, 0, keepdims=False)
    theirs = lax.dynamic_index_in_dim(array, 1 - core, 0, keepdims=False)
    arrived = swap_cores(theirs)
    both = (mine.astype(F32) + arrived.astype(F32)).astype(BF16)
    spread = lax.all_to_all(both, "seq", 0, 0, axis_index_groups=PLANE, tiled=True)
    return jnp.sum(spread.astype(F32), axis=0)


def reduce_dp(array):
    spread = lax.all_to_all(array.astype(BF16), "dp", 0, 0, tiled=True)
    return jnp.sum(spread.astype(F32), axis=0)


def pad_last(array, size):
    return jnp.pad(array, [(0, 0)] * (array.ndim - 1) + [(0, size - array.shape[-1])])


def pad_groups(array):
    groups = array.reshape(array.shape[:-1] + (array.shape[-1] // 30, 30))
    return pad_last(groups, 32).reshape(array.shape[:-1] + (-1,))


def drop_groups(array):
    groups = array.reshape(array.shape[:-1] + (array.shape[-1] // 32, 32))
    return groups[..., :30].reshape(array.shape[:-1] + (-1,))


def to_tiles(array, rows):
    array = jnp.pad(array, ((0, rows - array.shape[0]), (0, 0)))
    count = array.shape[1] // 128
    return array.reshape(rows, count, 128).transpose(1, 0, 2).reshape(count * rows, 128)


def from_tiles(array, rows):
    count = array.shape[0] // rows
    return array.reshape(count, rows, 128).transpose(1, 0, 2).reshape(rows, count * 128)


def on_device(inputs, w_project, w_output, w_expand, w_contract, norm_gains, segments, cotangent):
    tok = inputs.shape[1]
    layers = 2
    local_segment = segments[0]

    pieces = [to_tiles(pad_groups(w_expand[layer].T), 160) for layer in range(layers)]
    pieces += [to_tiles(w_contract[layer].T, 32) for layer in range(layers)]
    pieces += [to_tiles(pad_last(w_output[layer].T, 256), 32) for layer in range(layers)]
    pieces += [to_tiles(pad_groups(w_project[1].T), 64)]
    bulk = lax.all_gather(jnp.concatenate(pieces, axis=0), ("dp", "seq"))
    bulk = bulk.reshape((4, 32) + bulk.shape[1:])

    extra = jnp.zeros((LEAD - PROJECT - 2, 128), BF16)
    lead = jnp.concatenate(
        [
            to_tiles(pad_groups(w_project[0].T), 64),
            pad_last(norm_gains[None, :], 128),
            local_segment.astype(BF16)[None, :],
            extra,
        ],
        axis=0,
    )
    leads = lax.all_gather(lead, "dp").reshape(2, 2, LEAD, 128)
    leads = gather_seq(leads).reshape(32, 4, LEAD, 128)
    gains = leads[:, :, PROJECT, :32].transpose(1, 0, 2).reshape(4, 1, PADDED).astype(F32)
    all_segment = lax.dynamic_index_in_dim(
        leads[:, :, PROJECT + 1, :], lax.axis_index("dp"), 1, keepdims=False
    )
    all_segment = all_segment.reshape(-1).astype(jnp.int32)
    length = all_segment.shape[0]
    projects = [
        leads[:, :, :PROJECT].transpose(1, 0, 2, 3),
        bulk[:, :, 2 * GRADS : 2 * GRADS + PROJECT],
    ]

    query_index = lax.axis_index("seq") * tok + jnp.arange(tok, dtype=jnp.int32)
    key_index = jnp.arange(length, dtype=jnp.int32)
    starts = jnp.sum((all_segment[:, None] < local_segment[None, :]).astype(jnp.int32), axis=0)
    position = (query_index - starts).astype(F32)
    angle = frequencies(HEAD)[:, None] * position[None, :]
    cosine = jnp.cos(angle)
    sine = jnp.sin(angle)
    allowed = (local_segment[None, :] == all_segment[:, None]) & (
        query_index[None, :] >= key_index[:, None]
    )
    bias = jnp.where(allowed, 0.0, MASKED).astype(F32)
    chunk_range = jnp.stack([starts[0] // CHUNK, query_index[-1] // CHUNK + 1])

    stream = pad_groups(inputs[0]).astype(F32)
    records = []
    for layer in range(layers):
        queries, packed_local, normed = project_forward(
            stream, gains[2 * layer], projects[layer], cosine, sine
        )
        packed = gather_seq(packed_local.reshape(2, tok // 2, 2 * KVD)).reshape(length, 2 * KVD)
        mixed_wide, log_total = attend_forward(queries, packed, bias, chunk_range)
        mixed, middle, normed_feed, gate, up, hidden, after = feed_forward(
            stream, mixed_wide, gains[2 * layer + 1], bulk, layer
        )
        records.append(
            (stream, queries, packed, normed, mixed_wide, log_total)
            + (mixed, middle, normed_feed, gate, up, hidden)
        )
        stream = after
    block_output = drop_groups(stream.astype(BF16))[None]

    grad_stream = pad_groups(cotangent[0]).astype(F32)
    gain_grads = [None] * 4
    bulk_grads = [None] * layers
    project = None
    for layer in reversed(range(layers)):
        stream_in, queries, packed, normed, mixed_wide, log_total = records[layer][:6]
        mixed, middle, normed_feed, gate, up, hidden = records[layer][6:]
        grad_low, grad_gate, grad_up, grad_middle, middle_low, gain_grad, grad_mixed, inner = (
            feed_backward(
                grad_stream, middle, gains[2 * layer + 1], mixed_wide, gate, up, bulk, layer
            )
        )
        gain_grads[2 * layer + 1] = gain_grad
        payload = weight_gradients(
            grad_gate, grad_up, normed_feed, grad_low, hidden, middle_low, mixed, project
        )
        bulk_grads[layer] = lax.psum_scatter(payload, "seq", scatter_dimension=0)
        grad_query, grad_packed = attend_backward(
            queries, packed, bias, chunk_range, log_total, inner, grad_mixed
        )
        grad_local = reduce_seq(grad_packed)
        padded, grad_stream, gain_grad = project_backward(
            grad_query,
            grad_local,
            cosine,
            sine,
            projects[layer],
            stream_in,
            gains[2 * layer],
            grad_middle,
        )
        gain_grads[2 * layer] = gain_grad
        project = (padded, normed)

    gain_rows = jnp.concatenate(gain_grads, axis=0).astype(BF16).reshape(4, 32, 32)
    gain_rows = gain_rows.transpose(1, 0, 2)[:, :, None, :]
    gain_rows = jnp.pad(gain_rows, ((0, 0), (0, 0), (0, LEAD - PROJECT - 1), (0, 96)))
    second = reduce_dp(bulk_grads[1])
    lead_grads, second = lax.optimization_barrier(
        (lead_gradients(padded, normed, gain_rows), second)
    )
    small = reduce_seq(lead_grads)
    first = reduce_dp(jnp.concatenate([bulk_grads[0], small.astype(BF16)], axis=1))
    parts = [first, second]
    last_part = first[GRADS : GRADS + PROJECT]
    lead_part = first[GRADS + PROJECT :]

    def project_out(tile_rows):
        return drop_groups(from_tiles(tile_rows, 64)[:50]).T

    expand_out = jnp.stack([drop_groups(from_tiles(part[:EXPAND], 160)).T for part in parts])
    contract_out = jnp.stack(
        [from_tiles(part[EXPAND : EXPAND + CONTRACT], 32)[:30].T for part in parts]
    )
    output_out = jnp.stack(
        [from_tiles(part[EXPAND + CONTRACT : GRADS], 32)[:30, :240].T for part in parts]
    )
    return (
        block_output,
        drop_groups(grad_stream)[None],
        jnp.stack([project_out(lead_part[:PROJECT]), project_out(last_part)]),
        output_out,
        expand_out,
        contract_out,
        lead_part[PROJECT, :30],
    )


def solution(mesh):
    in_specs = (
        P("dp", "seq", None),
        P(None, "dp", "seq"),
        P(None, "dp", "seq"),
        P(None, "dp", "seq"),
        P(None, "dp", "seq"),
        P(("dp", "seq")),
        P("dp", "seq"),
        P("dp", "seq", None),
    )
    out_specs = (
        P("dp", "seq", None),
        P("dp", "seq", None),
        P(None, "dp", "seq"),
        P(None, "dp", "seq"),
        P(None, "dp", "seq"),
        P(None, "dp", "seq"),
        P(("dp", "seq")),
    )
    return jax.shard_map(
        on_device, mesh=mesh, in_specs=in_specs, out_specs=out_specs, check_vma=False
    )
```

```python
import functools
import math

import jax
import jax.numpy as jnp
from jax import lax
from jax.experimental import pallas as pl
from jax.experimental.pallas import tpu as pltpu
from jax.sharding import PartitionSpec as P

HEADS = 15
KV_HEADS = 5
HEAD = 64
GROUP = HEADS // KV_HEADS
KVD = KV_HEADS * HEAD
WIDTH = 960
FF = 2560

EPSILON = 1e-05
THETA = 100000.0
MASKED = -1e30

RING_Y = [[z * 8 + y * 2 + c for y in range(4)] for z in range(4) for c in range(2)]
PLANE = [[i * 2 + c for i in range(16)] for c in range(2)]
SWAP = [(i, i ^ 1) for i in range(32)]

PADDED = 1024
EXPAND = 320
CONTRACT = 160
OUTPUT = 64
PROJECT = 128
LEAD = 144
GRADS = EXPAND + CONTRACT + OUTPUT
CHUNK = 512
LIMIT = 40 << 20

F32 = jnp.float32
BF16 = jnp.bfloat16
IN_VMEM = pl.BlockSpec(memory_space=pltpu.VMEM)
IN_SMEM = pl.BlockSpec(memory_space=pltpu.SMEM)


def shape(dims, dtype):
    return jax.ShapeDtypeStruct(dims, dtype)


def params():
    return pltpu.CompilerParams(vmem_limit_bytes=LIMIT)


def cost(flops, traffic):
    return pl.CostEstimate(flops=flops, bytes_accessed=traffic, transcendentals=0)


def nn_dot(left, right):
    return jnp.dot(left, right, preferred_element_type=F32)


def nt_dot(left, right):
    return lax.dot_general(left, right, (((1,), (1,)), ((), ())), preferred_element_type=F32)


def tn_dot(left, right):
    return lax.dot_general(left, right, (((0,), (0,)), ((), ())), preferred_element_type=F32)


def frequencies(size):
    half = size // 2
    return 1.0 / THETA ** (jnp.arange(half, dtype=F32) * 2.0 / size)


def norm_scale(stream):
    return lax.rsqrt(jnp.sum(stream * stream, axis=1, keepdims=True) / WIDTH + EPSILON)


def norm_pull(stream, gain, grad):
    scale = norm_scale(stream)
    weighted = gain * grad
    mean = jnp.sum(weighted * stream, axis=1, keepdims=True) / WIDTH
    grad_stream = scale * weighted - stream * (scale * scale * scale * mean)
    return grad_stream, jnp.sum(grad * stream * scale, axis=0, keepdims=True)


def tiles(ref, devices, start, rows, count, first):
    pieces = []
    for dp in range(ref.shape[0]):
        for tile in range(count):
            at = first + tile * rows
            block = ref[dp, start : start + devices, at : at + rows, :]
            pieces.append(block.reshape(devices * rows, 128))
    return jnp.concatenate(pieces, axis=1)


def project_specs(layer):
    if layer == 0:
        return [
            pl.BlockSpec((32, 4, 64, 128), lambda j: (0, 0, 0, 0)),
            pl.BlockSpec((32, 4, 64, 128), lambda j: (0, 0, 1, 0)),
        ]
    first = 2 * GRADS // 64
    return [
        pl.BlockSpec((4, 32, 64, 128), lambda j: (0, 0, first, 0)),
        pl.BlockSpec((4, 32, 64, 128), lambda j: (0, 0, first + 1, 0)),
    ]


def project_tiles(pair, start):
    pieces = []
    for dp in range(4):
        for ref in pair:
            if ref.shape[0] == 32:
                block = ref[start : start + 8, dp]
            else:
                block = ref[dp, start : start + 8]
            pieces.append(block.reshape(512, 128))
    return jnp.concatenate(pieces, axis=1)


def project_kernel(stream_ref, gain_ref, weight_one, weight_two, cosine_ref, sine_ref, *rest):
    query_ref, packed_ref, normed_ref, natural = rest
    stream = stream_ref[...]
    normed = (stream * norm_scale(stream) * gain_ref[...]).astype(BF16)
    normed_ref[...] = normed
    for part in range(4):
        result = nt_dot(project_tiles((weight_one, weight_two), part * 8), normed)
        for s in range(8):
            at = part * 8 + s
            natural[at * 50 : at * 50 + 50, :] = result[s * 64 : s * 64 + 50, :]
    cosine, sine = cosine_ref[...], sine_ref[...]
    for head in range(HEADS + KV_HEADS):
        at = head * HEAD
        first = natural[at : at + 32, :]
        second = natural[at + 32 : at + 64, :]
        one = first * cosine - second * sine
        two = second * cosine + first * sine
        if head < HEADS:
            both = jnp.concatenate([one, two], axis=0) * (1.0 / math.sqrt(HEAD))
            query_ref[at : at + 64, :] = both.astype(BF16)
        else:
            natural[at : at + 32, :] = one
            natural[at + 32 : at + 64, :] = two
    packed_ref[...] = natural[WIDTH : WIDTH + 2 * KVD, :].T.astype(BF16)


def project_forward(stream, gain, weight, layer, cosine, sine):
    tok = stream.shape[0]
    return pl.pallas_call(
        project_kernel,
        grid=(1,),
        out_shape=(
            shape((WIDTH, tok), BF16),
            shape((tok, 2 * KVD), BF16),
            shape((tok, PADDED), BF16),
        ),
        in_specs=[whole((tok, PADDED)), whole((1, PADDED))]
        + project_specs(layer)
        + [whole((32, tok)), whole((32, tok))],
        out_specs=(whole((WIDTH, tok)), whole((tok, 2 * KVD)), whole((tok, PADDED))),
        scratch_shapes=[pltpu.VMEM((WIDTH + 2 * KVD, tok), F32)],
        compiler_params=params(),
        cost_estimate=cost(2 * tok * 2048 * 1024, 5 << 20),
    )(stream, gain, weight, weight, cosine, sine)


def take_heads(ref, head):
    return jnp.concatenate(
        [ref[(GROUP * head + g) * HEAD : (GROUP * head + g + 1) * HEAD, :] for g in range(GROUP)],
        axis=1,
    )


def take_row(ref, head):
    return jnp.concatenate(
        [ref[GROUP * head + g : GROUP * head + g + 1, :] for g in range(GROUP)], axis=1
    )


def forward_kernel(
    range_ref, query_ref, packed_ref, bias_ref, mixed_ref, total_ref, top, total, mixed
):
    tok = query_ref.shape[1]
    top[...] = jnp.full(top.shape, MASKED, F32)
    total[...] = jnp.zeros(total.shape, F32)
    mixed[...] = jnp.zeros(mixed.shape, F32)

    def step(index, carry):
        rows = pl.ds(pl.multiple_of(index * CHUNK, CHUNK), CHUNK)
        bias = jnp.concatenate([bias_ref[rows, :]] * GROUP, axis=1)

        def scores_of(head):
            key = packed_ref[rows, head * HEAD : (head + 1) * HEAD]
            return nn_dot(key, take_heads(query_ref, head)) + bias

        later = scores_of(0)
        for head in range(KV_HEADS):
            scores = later
            if head + 1 < KV_HEADS:
                later = scores_of(head + 1)
            value = packed_ref[rows, KVD + head * HEAD : KVD + (head + 1) * HEAD]
            old_top = top[head]
            new_top = jnp.maximum(old_top, jnp.max(scores, axis=0, keepdims=True))
            raised = jnp.exp(scores - new_top)
            shrink = jnp.exp(old_top - new_top)
            top[head] = new_top
            total[head] = total[head] * shrink + jnp.sum(raised, axis=0, keepdims=True)
            mixed[head] = mixed[head] * shrink + tn_dot(value, raised.astype(BF16))
        return carry

    lax.fori_loop(range_ref[0], range_ref[1], step, 0)
    for head in range(KV_HEADS):
        result = mixed[head] / total[head]
        log_total = top[head] + jnp.log(total[head])
        for g in range(GROUP):
            at = GROUP * head + g
            columns = slice(g * tok, (g + 1) * tok)
            mixed_ref[at * HEAD : (at + 1) * HEAD, :] = result[:, columns]
            total_ref[at : at + 1, :] = log_total[:, columns]


def attend_forward(queries, packed, bias, chunk_range):
    tok = queries.shape[1]
    return pl.pallas_call(
        forward_kernel,
        out_shape=(shape((WIDTH, tok), F32), shape((HEADS, tok), F32)),
        in_specs=[IN_SMEM] + [IN_VMEM] * 3,
        out_specs=(IN_VMEM, IN_VMEM),
        scratch_shapes=[
            pltpu.VMEM((KV_HEADS, 1, GROUP * tok), F32),
            pltpu.VMEM((KV_HEADS, 1, GROUP * tok), F32),
            pltpu.VMEM((KV_HEADS, HEAD, GROUP * tok), F32),
        ],
        compiler_params=params(),
        cost_estimate=cost(4 * 4096 * 128 * 960, 8 << 20),
    )(chunk_range, queries, packed, bias)


def backward_kernel(
    range_ref,
    query_ref,
    packed_ref,
    bias_ref,
    total_ref,
    inner_ref,
    grad_ref,
    query_out,
    packed_out,
    grad_query,
):
    tok = query_ref.shape[1]
    packed_out[...] = jnp.zeros(packed_out.shape, packed_out.dtype)
    grad_query[...] = jnp.zeros(grad_query.shape, F32)

    def step(index, carry):
        rows = pl.ds(pl.multiple_of(index * CHUNK, CHUNK), CHUNK)
        bias = jnp.concatenate([bias_ref[rows, :]] * GROUP, axis=1)

        def products(head):
            key = packed_ref[rows, head * HEAD : (head + 1) * HEAD]
            value = packed_ref[rows, KVD + head * HEAD : KVD + (head + 1) * HEAD]
            scores = nn_dot(key, take_heads(query_ref, head)) + bias
            return key, scores, nn_dot(value, take_heads(grad_ref, head))

        later = products(0)
        for head in range(KV_HEADS):
            key, scores, grad_chance = later
            if head + 1 < KV_HEADS:
                later = products(head + 1)
            chance = jnp.exp(scores - take_row(total_ref, head))
            grad_scores = (chance * (grad_chance - take_row(inner_ref, head))).astype(BF16)
            grad_key = nt_dot(grad_scores, take_heads(query_ref, head)).astype(BF16)
            grad_value = nt_dot(chance.astype(BF16), take_heads(grad_ref, head)).astype(BF16)
            key_lanes = slice(head * HEAD, (head + 1) * HEAD)
            value_lanes = slice(KVD + head * HEAD, KVD + (head + 1) * HEAD)
            for block in range(CHUNK // tok):
                at = index * (CHUNK // tok // 2) + block // 2
                part = slice(block * tok, (block + 1) * tok)
                packed_out[block % 2, at, :, key_lanes] = grad_key[part, :]
                packed_out[block % 2, at, :, value_lanes] = grad_value[part, :]
            grad_query[head] += tn_dot(key, grad_scores)
        return carry

    lax.fori_loop(range_ref[0], range_ref[1], step, 0)
    for head in range(KV_HEADS):
        result = grad_query[head] * (1.0 / math.sqrt(HEAD))
        for g in range(GROUP):
            at = GROUP * head + g
            query_out[at * HEAD : (at + 1) * HEAD, :] = result[:, g * tok : (g + 1) * tok]


def attend_backward(queries, packed, bias, chunk_range, log_total, inner, grad_mixed):
    tok = queries.shape[1]
    return pl.pallas_call(
        backward_kernel,
        out_shape=(shape((WIDTH, tok), F32), shape((2, 16, tok, 2 * KVD), BF16)),
        in_specs=[IN_SMEM] + [IN_VMEM] * 6,
        out_specs=(IN_VMEM, IN_VMEM),
        scratch_shapes=[pltpu.VMEM((KV_HEADS, HEAD, GROUP * tok), F32)],
        compiler_params=params(),
        cost_estimate=cost(10 * 4096 * 128 * 960, 13 << 20),
    )(chunk_range, queries, packed, bias, log_total, inner, grad_mixed)


def feed_kernel(
    stream_ref, mixed_ref, gain_ref, output_ref, gate_w, up_w, contract_w, *rest
):
    mixed_out, middle_out, normed_out, gate_out, up_out, hidden_out, stream_out = rest
    tok = stream_ref.shape[0]

    @pl.when(pl.program_id(0) == 0)
    def _():
        pieces = []
        for dp in range(4):
            pieces += [mixed_ref[dp * 240 : dp * 240 + 240, :], jnp.zeros((16, tok), F32)]
        mixed = jnp.concatenate(pieces, axis=0).T.astype(BF16)
        mixed_out[...] = mixed
        middle = stream_ref[...] + nt_dot(mixed, tiles(output_ref, 32, 0, 32, 2, 0))
        middle_out[...] = middle
        normed_out[...] = (middle * norm_scale(middle) * gain_ref[...]).astype(BF16)
        stream_out[...] = middle

    normed = normed_out[...]
    gate = nt_dot(normed, tiles(gate_w, 4, 0, 160, 2, 0))
    up = nt_dot(normed, tiles(up_w, 4, 0, 160, 2, 0))
    gate_out[...] = gate
    up_out[...] = up
    hidden = (gate / (1.0 + jnp.exp(-gate)) * up).astype(BF16)
    hidden_out[...] = hidden
    stream_out[...] += nt_dot(hidden, tiles(contract_w, 32, 0, 32, 5, 0))


def whole(dims):
    return pl.BlockSpec(dims, lambda j: (0,) * len(dims))


def weight_specs(layer):
    return [
        pl.BlockSpec((4, 32, OUTPUT, 128), lambda j: (0, 0, 15 + layer, 0)),
        pl.BlockSpec((4, 4, EXPAND, 128), lambda j: (0, j, layer, 0)),
        pl.BlockSpec((4, 4, EXPAND, 128), lambda j: (0, j + 4, layer, 0)),
        pl.BlockSpec((1, 32, CONTRACT, 128), lambda j: (j, 0, 4 + layer, 0)),
    ]


def feed_forward(stream, mixed, gain, bulk, layer):
    tok = stream.shape[0]
    column = pl.BlockSpec((tok, 640), lambda j: (0, j))
    return pl.pallas_call(
        feed_kernel,
        grid=(4,),
        out_shape=(
            shape((tok, PADDED), BF16),
            shape((tok, PADDED), F32),
            shape((tok, PADDED), BF16),
            shape((tok, FF), F32),
            shape((tok, FF), F32),
            shape((tok, FF), BF16),
            shape((tok, PADDED), F32),
        ),
        in_specs=[whole((tok, PADDED)), whole((WIDTH, tok)), whole((1, PADDED))]
        + weight_specs(layer),
        out_specs=(whole((tok, PADDED)),) * 3 + (column,) * 3 + (whole((tok, PADDED)),),
        compiler_params=params(),
        cost_estimate=cost(2 * tok * 9000 * 1024, 18 << 20),
    )(stream, mixed, gain, bulk, bulk, bulk, bulk)


def feed_pull_kernel(
    grad_ref,
    middle_ref,
    gain_ref,
    mixed_ref,
    gate_ref,
    up_ref,
    output_ref,
    gate_w,
    up_w,
    contract_w,
    *rest,
):
    low_out, gate_up_out, middle_out, middle_low_out, gain_out, mixed_out, inner_out, total = rest
    index = pl.program_id(0)
    tok = grad_ref.shape[0]

    @pl.when(index == 0)
    def _():
        low_out[...] = grad_ref[...].astype(BF16)
        total[...] = jnp.zeros_like(total)

    gate, up = gate_ref[...], up_ref[...]
    grad_hidden = nn_dot(low_out[...], tiles(contract_w, 32, 0, 32, 5, 0))
    chance = 1.0 / (1.0 + jnp.exp(-gate))
    swish = gate * chance
    grad_gate = (grad_hidden * up * (chance + swish * (1.0 - chance))).astype(BF16)
    grad_up = (grad_hidden * swish).astype(BF16)
    gate_up_out[0] = grad_gate
    gate_up_out[1] = grad_up
    total[...] += nn_dot(grad_gate, tiles(gate_w, 4, 0, 160, 2, 0)) + nn_dot(
        grad_up, tiles(up_w, 4, 0, 160, 2, 0)
    )

    @pl.when(index == pl.num_programs(0) - 1)
    def _():
        grad_part, grad_gain = norm_pull(middle_ref[...], gain_ref[...], total[...])
        grad_middle = grad_ref[...] + grad_part
        middle_out[...] = grad_middle
        gain_out[...] = grad_gain
        low = grad_middle.astype(BF16)
        middle_low_out[...] = low
        back = nn_dot(low, tiles(output_ref, 32, 0, 32, 2, 0)).astype(BF16).astype(F32).T
        for dp in range(4):
            mixed_out[dp * 240 : dp * 240 + 240, :] = back[dp * 256 : dp * 256 + 240, :].astype(BF16)
        for head in range(HEADS):
            rows = slice(head * HEAD, head * HEAD + HEAD)
            product = mixed_out[rows, :].astype(F32) * mixed_ref[rows, :]
            inner_out[head : head + 1, :] = jnp.sum(product, axis=0, keepdims=True)


def feed_backward(grad, middle, gain, mixed, gate, up, bulk, layer):
    tok = grad.shape[0]
    column = pl.BlockSpec((tok, 640), lambda j: (0, j))
    return pl.pallas_call(
        feed_pull_kernel,
        grid=(4,),
        out_shape=(
            shape((tok, PADDED), BF16),
            shape((2, tok, FF), BF16),
            shape((tok, PADDED), F32),
            shape((tok, PADDED), BF16),
            shape((1, PADDED), F32),
            shape((WIDTH, tok), BF16),
            shape((HEADS, tok), F32),
        ),
        in_specs=[
            whole((tok, PADDED)),
            whole((tok, PADDED)),
            whole((1, PADDED)),
            whole((WIDTH, tok)),
            column,
            column,
        ]
        + weight_specs(layer),
        out_specs=(
            whole((tok, PADDED)),
            pl.BlockSpec((2, tok, 640), lambda j: (0, 0, j)),
            whole((tok, PADDED)),
            whole((tok, PADDED)),
            whole((1, PADDED)),
            whole((WIDTH, tok)),
            whole((HEADS, tok)),
        ),
        scratch_shapes=[pltpu.VMEM((tok, PADDED), F32)],
        compiler_params=params(),
        cost_estimate=cost(2 * tok * 9000 * 1024, 18 << 20),
    )(grad, middle, gain, mixed, gate, up, bulk, bulk, bulk, bulk)


def put_tiles(out_ref, result, rows, count, first):
    for dp in range(4):
        for tile in range(count):
            at = (dp * count + tile) * 128
            block = result[:, at : at + 128].reshape(4, rows, 128).astype(BF16)
            out_ref[:, dp, first + tile * rows : first + (tile + 1) * rows, :] = block


def weight_kernel(with_project, *refs):
    gate_ref, normed_ref, low_ref, hidden_ref, middle_ref, mixed_ref = refs[:6]
    out_ref = refs[-1]
    put_tiles(out_ref, tn_dot(gate_ref[0], normed_ref[...]), 160, 2, 0)
    put_tiles(out_ref, tn_dot(low_ref[...], hidden_ref[...]), 32, 5, EXPAND)
    put_tiles(out_ref, tn_dot(middle_ref[...], mixed_ref[...]), 32, 2, EXPAND + CONTRACT)
    if with_project:
        put_tiles(out_ref, nn_dot(refs[6][...], refs[7][...]), 64, 2, GRADS)


def weight_gradients(grad_gate_up, normed_feed, grad_low, hidden, middle_low, mixed, project):
    tok = normed_feed.shape[0]
    rows = GRADS + (PROJECT if project else 0)
    operands = [grad_gate_up, normed_feed, grad_low, hidden, middle_low, mixed]
    in_specs = [
        pl.BlockSpec((1, tok, 640), lambda j: (j // 4, 0, j % 4)),
        whole((tok, PADDED)),
        pl.BlockSpec((tok, 128), lambda j: (0, j)),
        whole((tok, FF)),
        pl.BlockSpec((tok, 128), lambda j: (0, j)),
        whole((tok, PADDED)),
    ]
    if project:
        operands += list(project)
        in_specs += [pl.BlockSpec((256, tok), lambda j: (j, 0)), whole((tok, PADDED))]
    return pl.pallas_call(
        functools.partial(weight_kernel, bool(project)),
        grid=(8,),
        out_shape=shape((32, 4, rows, 128), BF16),
        in_specs=in_specs,
        out_specs=pl.BlockSpec((4, 4, rows, 128), lambda j: (j, 0, 0, 0)),
        compiler_params=params(),
        cost_estimate=cost(2 * tok * 11000 * 1024, 20 << 20),
    )(*operands)


def project_pull_kernel(
    query_ref,
    local_ref,
    cosine_ref,
    sine_ref,
    weight_one,
    weight_two,
    stream_ref,
    gain_ref,
    grad_ref,
    *rest,
):
    padded_out, grad_out, gain_out, natural, spread = rest
    tok = stream_ref.shape[0]
    natural[0:WIDTH, :] = query_ref[...]
    natural[WIDTH : WIDTH + 2 * KVD, :] = local_ref[...].T
    cosine, sine = cosine_ref[...], sine_ref[...]
    for head in range(HEADS + KV_HEADS):
        at = head * HEAD
        first = natural[at : at + 32, :]
        second = natural[at + 32 : at + 64, :]
        natural[at : at + 32, :] = first * cosine + second * sine
        natural[at + 32 : at + 64, :] = second * cosine - first * sine
    for s in range(32):
        spread[s * 64 : s * 64 + 50, :] = natural[s * 50 : s * 50 + 50, :]
        spread[s * 64 + 50 : s * 64 + 64, :] = jnp.zeros((14, tok), F32)
    total = jnp.zeros((tok, PADDED), F32)
    for part in range(4):
        block = spread[part * 512 : (part + 1) * 512, :].astype(BF16)
        padded_out[part * 512 : (part + 1) * 512, :] = block
        total = total + tn_dot(block, project_tiles((weight_one, weight_two), part * 8))
    grad_part, grad_gain = norm_pull(stream_ref[...], gain_ref[...], total)
    grad_out[...] = grad_ref[...] + grad_part
    gain_out[...] = grad_gain


def project_backward(grad_query, grad_local, cosine, sine, weight, layer, stream, gain, grad_middle):
    tok = stream.shape[0]
    return pl.pallas_call(
        project_pull_kernel,
        grid=(1,),
        out_shape=(
            shape((2048, tok), BF16),
            shape((tok, PADDED), F32),
            shape((1, PADDED), F32),
        ),
        in_specs=[
            whole((WIDTH, tok)),
            whole((tok, 2 * KVD)),
            whole((32, tok)),
            whole((32, tok)),
        ]
        + project_specs(layer)
        + [whole((tok, PADDED)), whole((1, PADDED)), whole((tok, PADDED))],
        out_specs=(whole((2048, tok)), whole((tok, PADDED)), whole((1, PADDED))),
        scratch_shapes=[
            pltpu.VMEM((WIDTH + 2 * KVD, tok), F32),
            pltpu.VMEM((2048, tok), F32),
        ],
        compiler_params=params(),
        cost_estimate=cost(2 * tok * 2048 * 1024, 6 << 20),
    )(grad_query, grad_local, cosine, sine, weight, weight, stream, gain, grad_middle)


def lead_kernel(padded_ref, normed_ref, gains_ref, out_ref):
    result = nn_dot(padded_ref[...], normed_ref[...])
    for dp in range(4):
        for tile in range(2):
            at = (dp * 2 + tile) * 128
            block = result[:, at : at + 128].reshape(2, 2, 64, 128).astype(BF16)
            for core in range(2):
                out_ref[core, :, dp, tile * 64 : tile * 64 + 64, :] = block[:, core]
    for core in range(2):
        for place in range(2):
            out_ref[core, place, :, PROJECT:LEAD, :] = gains_ref[place * 2 + core]


def lead_gradients(padded, normed, gains):
    tok = normed.shape[0]
    return pl.pallas_call(
        lead_kernel,
        grid=(8,),
        out_shape=shape((2, 16, 4, LEAD, 128), BF16),
        in_specs=[
            pl.BlockSpec((256, tok), lambda j: (j, 0)),
            whole((tok, PADDED)),
            pl.BlockSpec((4, 4, LEAD - PROJECT, 128), lambda j: (j, 0, 0, 0)),
        ],
        out_specs=pl.BlockSpec((2, 2, 4, LEAD, 128), lambda j: (0, j, 0, 0, 0)),
        compiler_params=params(),
        cost_estimate=cost(2 * tok * 2048 * 1024, 6 << 20),
    )(padded, normed, gains)


def swap_cores(array):
    return lax.ppermute(array, "seq", SWAP)


def hop_y(array, hop):
    moves = [(i, i // 8 * 8 + (i % 8 + 2 * hop) % 8) for i in range(32)]
    return lax.ppermute(array, "seq", moves)


def hop_z(array, hop):
    return lax.ppermute(array, "seq", [(i, (i + 8 * hop) % 32) for i in range(32)])


def ring(array, move):
    return jnp.stack([array] + [move(array, hop) for hop in (1, 2, 3)])


def order_kernel(place_ref, first_own, last_own, first_other, last_other, out_ref):
    for s in range(32):
        back_z = lax.rem(place_ref[0] - s // 8 + 4, 4)
        back_y = lax.rem(place_ref[1] - s // 2 % 4 + 4, 4)
        same = place_ref[2] == s % 2

        @pl.when(same)
        def _(s=s, back_z=back_z, back_y=back_y):
            out_ref[s, 0] = first_own[back_z, back_y]
            out_ref[s, 1] = last_own[back_y, back_z]

        @pl.when(jnp.logical_not(same))
        def _(s=s, back_z=back_z, back_y=back_y):
            out_ref[s, 0] = first_other[back_z, back_y]
            out_ref[s, 1] = last_other[back_y, back_z]


def gather_seq(array):
    index = lax.axis_index("seq")
    first = ring(array[0], hop_y)
    last = ring(array[1], hop_z)
    first = ring(first, hop_z)
    last = ring(last, hop_y)
    place = jnp.stack([index // 8, index // 2 % 4, index % 2]).astype(jnp.int32)
    return pl.pallas_call(
        order_kernel,
        out_shape=shape((32,) + array.shape, array.dtype),
        in_specs=[IN_SMEM] + [IN_VMEM] * 4,
        out_specs=IN_VMEM,
        compiler_params=params(),
        cost_estimate=cost(0, 12 << 20),
    )(place, first, last, swap_cores(first), swap_cores(last))


def reduce_seq(array):
    core = lax.axis_index("seq") % 2
    mine = lax.dynamic_index_in_dim(array, core, 0, keepdims=False)
    theirs = lax.dynamic_index_in_dim(array, 1 - core, 0, keepdims=False)
    arrived = swap_cores(theirs)
    both = (mine.astype(F32) + arrived.astype(F32)).astype(BF16)
    spread = lax.all_to_all(both, "seq", 0, 0, axis_index_groups=PLANE, tiled=True)
    return jnp.sum(spread.astype(F32), axis=0)


def reduce_dp(array):
    array = array.astype(BF16)
    place = lax.axis_index("dp")
    total = lax.dynamic_index_in_dim(array, place, 0, keepdims=False).astype(F32)
    for hop in (1, 2, 3):
        block = lax.dynamic_index_in_dim(array, (place + hop) % 4, 0, keepdims=False)
        moved = lax.ppermute(block, "dp", [(i, (i + hop) % 4) for i in range(4)])
        total = total + moved.astype(F32)
    return total


def pad_last(array, size):
    return jnp.pad(array, [(0, 0)] * (array.ndim - 1) + [(0, size - array.shape[-1])])


def pad_groups(array):
    groups = array.reshape(array.shape[:-1] + (array.shape[-1] // 30, 30))
    return pad_last(groups, 32).reshape(array.shape[:-1] + (-1,))


def drop_groups(array):
    groups = array.reshape(array.shape[:-1] + (array.shape[-1] // 32, 32))
    return groups[..., :30].reshape(array.shape[:-1] + (-1,))


def to_tiles(array, rows):
    array = jnp.pad(array, ((0, rows - array.shape[0]), (0, 0)))
    count = array.shape[1] // 128
    return array.reshape(rows, count, 128).transpose(1, 0, 2).reshape(count * rows, 128)


def from_tiles(array, rows):
    count = array.shape[0] // rows
    return array.reshape(count, rows, 128).transpose(1, 0, 2).reshape(rows, count * 128)


def on_device(inputs, w_project, w_output, w_expand, w_contract, norm_gains, segments, cotangent):
    tok = inputs.shape[1]
    layers = 2
    local_segment = segments[0]

    pieces = [to_tiles(pad_groups(w_expand[layer].T), 160) for layer in range(layers)]
    pieces += [to_tiles(w_contract[layer].T, 32) for layer in range(layers)]
    pieces += [to_tiles(pad_last(w_output[layer].T, 256), 32) for layer in range(layers)]
    pieces += [to_tiles(pad_groups(w_project[1].T), 64)]
    bulk = lax.all_gather(jnp.concatenate(pieces, axis=0), ("dp", "seq"))
    bulk = bulk.reshape((4, 32) + bulk.shape[1:])

    extra = jnp.zeros((LEAD - PROJECT - 2, 128), BF16)
    lead = jnp.concatenate(
        [
            to_tiles(pad_groups(w_project[0].T), 64),
            pad_last(norm_gains[None, :], 128),
            local_segment.astype(BF16)[None, :],
            extra,
        ],
        axis=0,
    )
    leads = lax.all_gather(lead, "dp").reshape(2, 2, LEAD, 128)
    leads = gather_seq(leads).reshape(32, 4, LEAD, 128)
    gains = leads[:, :, PROJECT, :32].transpose(1, 0, 2).reshape(4, 1, PADDED).astype(F32)
    all_segment = lax.dynamic_index_in_dim(
        leads[:, :, PROJECT + 1, :], lax.axis_index("dp"), 1, keepdims=False
    )
    all_segment = all_segment.reshape(-1).astype(jnp.int32)
    length = all_segment.shape[0]
    projects = [leads, bulk]

    query_index = lax.axis_index("seq") * tok + jnp.arange(tok, dtype=jnp.int32)
    key_index = jnp.arange(length, dtype=jnp.int32)
    starts = jnp.sum((all_segment[:, None] < local_segment[None, :]).astype(jnp.int32), axis=0)
    position = (query_index - starts).astype(F32)
    angle = frequencies(HEAD)[:, None] * position[None, :]
    cosine = jnp.cos(angle)
    sine = jnp.sin(angle)
    allowed = (local_segment[None, :] == all_segment[:, None]) & (
        query_index[None, :] >= key_index[:, None]
    )
    bias = jnp.where(allowed, 0.0, MASKED).astype(F32)
    chunk_range = jnp.stack([starts[0] // CHUNK, query_index[-1] // CHUNK + 1])

    stream = pad_groups(inputs[0]).astype(F32)
    records = []
    for layer in range(layers):
        queries, packed_local, normed = project_forward(
            stream, gains[2 * layer], projects[layer], layer, cosine, sine
        )
        packed = gather_seq(packed_local.reshape(2, tok // 2, 2 * KVD)).reshape(length, 2 * KVD)
        mixed_wide, log_total = attend_forward(queries, packed, bias, chunk_range)
        mixed, middle, normed_feed, gate, up, hidden, after = feed_forward(
            stream, mixed_wide, gains[2 * layer + 1], bulk, layer
        )
        records.append(
            (stream, queries, packed, normed, mixed_wide, log_total)
            + (mixed, middle, normed_feed, gate, up, hidden)
        )
        stream = after
    block_output = drop_groups(stream.astype(BF16))[None]

    grad_stream = pad_groups(cotangent[0]).astype(F32)
    gain_grads = [None] * 4
    bulk_grads = [None] * layers
    project = None
    for layer in reversed(range(layers)):
        stream_in, queries, packed, normed, mixed_wide, log_total = records[layer][:6]
        mixed, middle, normed_feed, gate, up, hidden = records[layer][6:]
        grad_low, grad_gate_up, grad_middle, middle_low, gain_grad, grad_mixed, inner = (
            feed_backward(
                grad_stream, middle, gains[2 * layer + 1], mixed_wide, gate, up, bulk, layer
            )
        )
        gain_grads[2 * layer + 1] = gain_grad
        payload = weight_gradients(
            grad_gate_up, normed_feed, grad_low, hidden, middle_low, mixed, project
        )
        bulk_grads[layer] = lax.psum_scatter(payload, "seq", scatter_dimension=0)
        grad_query, grad_packed = attend_backward(
            queries, packed, bias, chunk_range, log_total, inner, grad_mixed
        )
        grad_local = reduce_seq(grad_packed)
        padded, grad_stream, gain_grad = project_backward(
            grad_query,
            grad_local,
            cosine,
            sine,
            projects[layer],
            layer,
            stream_in,
            gains[2 * layer],
            grad_middle,
        )
        gain_grads[2 * layer] = gain_grad
        project = (padded, normed)

    gain_rows = jnp.concatenate(gain_grads, axis=0).astype(BF16).reshape(4, 32, 32)
    gain_rows = gain_rows.transpose(1, 0, 2)[:, :, None, :]
    gain_rows = jnp.pad(gain_rows, ((0, 0), (0, 0), (0, LEAD - PROJECT - 1), (0, 96)))
    second = reduce_dp(bulk_grads[1])
    lead_grads, second = lax.optimization_barrier(
        (lead_gradients(padded, normed, gain_rows), second)
    )
    lead_part = reduce_dp(reduce_seq(lead_grads))
    first = reduce_dp(bulk_grads[0])
    parts = [first, second]
    last_part = first[GRADS:]

    def project_out(tile_rows):
        return drop_groups(from_tiles(tile_rows, 64)[:50]).T

    expand_out = jnp.stack([drop_groups(from_tiles(part[:EXPAND], 160)).T for part in parts])
    contract_out = jnp.stack(
        [from_tiles(part[EXPAND : EXPAND + CONTRACT], 32)[:30].T for part in parts]
    )
    output_out = jnp.stack(
        [from_tiles(part[EXPAND + CONTRACT : GRADS], 32)[:30, :240].T for part in parts]
    )
    return (
        block_output,
        drop_groups(grad_stream)[None],
        jnp.stack([project_out(lead_part[:PROJECT]), project_out(last_part)]),
        output_out,
        expand_out,
        contract_out,
        lead_part[PROJECT, :30],
    )


def solution(mesh):
    in_specs = (
        P("dp", "seq", None),
        P(None, "dp", "seq"),
        P(None, "dp", "seq"),
        P(None, "dp", "seq"),
        P(None, "dp", "seq"),
        P(("dp", "seq")),
        P("dp", "seq"),
        P("dp", "seq", None),
    )
    out_specs = (
        P("dp", "seq", None),
        P("dp", "seq", None),
        P(None, "dp", "seq"),
        P(None, "dp", "seq"),
        P(None, "dp", "seq"),
        P(None, "dp", "seq"),
        P(("dp", "seq")),
    )
    return jax.shard_map(
        on_device, mesh=mesh, in_specs=in_specs, out_specs=out_specs, check_vma=False
    )
```

```python
import functools
import math

import jax
import jax.numpy as jnp
from jax import lax
from jax.experimental import pallas as pl
from jax.experimental.pallas import tpu as pltpu
from jax.sharding import PartitionSpec as P

HEADS = 15
KV_HEADS = 5
HEAD = 64
GROUP = HEADS // KV_HEADS
KVD = KV_HEADS * HEAD
WIDTH = 960
FF = 2560

EPSILON = 1e-05
THETA = 100000.0
MASKED = -1e30

RING_Y = [[z * 8 + y * 2 + c for y in range(4)] for z in range(4) for c in range(2)]
PLANE = [[i * 2 + c for i in range(16)] for c in range(2)]
SWAP = [(i, i ^ 1) for i in range(32)]

PADDED = 1024
EXPAND = 320
CONTRACT = 160
OUTPUT = 64
PROJECT = 128
LEAD = 144
GRADS = EXPAND + CONTRACT + OUTPUT
CHUNK = 512
LIMIT = 40 << 20

F32 = jnp.float32
BF16 = jnp.bfloat16
IN_VMEM = pl.BlockSpec(memory_space=pltpu.VMEM)
IN_SMEM = pl.BlockSpec(memory_space=pltpu.SMEM)


def shape(dims, dtype):
    return jax.ShapeDtypeStruct(dims, dtype)


def params():
    return pltpu.CompilerParams(vmem_limit_bytes=LIMIT)


def cost(flops, traffic):
    return pl.CostEstimate(flops=flops, bytes_accessed=traffic, transcendentals=0)


def nn_dot(left, right):
    return jnp.dot(left, right, preferred_element_type=F32)


def nt_dot(left, right):
    return lax.dot_general(left, right, (((1,), (1,)), ((), ())), preferred_element_type=F32)


def tn_dot(left, right):
    return lax.dot_general(left, right, (((0,), (0,)), ((), ())), preferred_element_type=F32)


def frequencies(size):
    half = size // 2
    return 1.0 / THETA ** (jnp.arange(half, dtype=F32) * 2.0 / size)


def norm_scale(stream):
    return lax.rsqrt(jnp.sum(stream * stream, axis=1, keepdims=True) / WIDTH + EPSILON)


def norm_pull(stream, gain, grad):
    scale = norm_scale(stream)
    weighted = gain * grad
    mean = jnp.sum(weighted * stream, axis=1, keepdims=True) / WIDTH
    grad_stream = scale * weighted - stream * (scale * scale * scale * mean)
    return grad_stream, jnp.sum(grad * stream * scale, axis=0, keepdims=True)


def tiles(ref, devices, start, rows, count, first):
    pieces = []
    for dp in range(ref.shape[0]):
        for tile in range(count):
            at = first + tile * rows
            block = ref[dp, start : start + devices, at : at + rows, :]
            pieces.append(block.reshape(devices * rows, 128))
    return jnp.concatenate(pieces, axis=1)


def project_specs(layer):
    if layer == 0:
        return [
            pl.BlockSpec((32, 4, 64, 128), lambda j: (0, 0, 0, 0)),
            pl.BlockSpec((32, 4, 64, 128), lambda j: (0, 0, 1, 0)),
        ]
    first = 2 * GRADS // 64
    return [
        pl.BlockSpec((4, 32, 64, 128), lambda j: (0, 0, first, 0)),
        pl.BlockSpec((4, 32, 64, 128), lambda j: (0, 0, first + 1, 0)),
    ]


def project_tiles(pair, start):
    pieces = []
    for dp in range(4):
        for ref in pair:
            if ref.shape[0] == 32:
                block = ref[start : start + 8, dp]
            else:
                block = ref[dp, start : start + 8]
            pieces.append(block.reshape(512, 128))
    return jnp.concatenate(pieces, axis=1)


def project_kernel(stream_ref, gain_ref, weight_one, weight_two, cosine_ref, sine_ref, *rest):
    query_ref, packed_ref, normed_ref, natural = rest
    stream = stream_ref[...]
    normed = (stream * norm_scale(stream) * gain_ref[...]).astype(BF16)
    normed_ref[...] = normed
    for part in range(4):
        result = nt_dot(project_tiles((weight_one, weight_two), part * 8), normed)
        for s in range(8):
            at = part * 8 + s
            natural[at * 50 : at * 50 + 50, :] = result[s * 64 : s * 64 + 50, :]
    cosine, sine = cosine_ref[...], sine_ref[...]
    for head in range(HEADS + KV_HEADS):
        at = head * HEAD
        first = natural[at : at + 32, :]
        second = natural[at + 32 : at + 64, :]
        one = first * cosine - second * sine
        two = second * cosine + first * sine
        if head < HEADS:
            both = jnp.concatenate([one, two], axis=0) * (1.0 / math.sqrt(HEAD))
            query_ref[at : at + 64, :] = both.astype(BF16)
        else:
            natural[at : at + 32, :] = one
            natural[at + 32 : at + 64, :] = two
    packed_ref[...] = natural[WIDTH : WIDTH + 2 * KVD, :].T.astype(BF16)


def project_forward(stream, gain, weight, layer, cosine, sine):
    tok = stream.shape[0]
    return pl.pallas_call(
        project_kernel,
        grid=(1,),
        out_shape=(
            shape((WIDTH, tok), BF16),
            shape((tok, 2 * KVD), BF16),
            shape((tok, PADDED), BF16),
        ),
        in_specs=[whole((tok, PADDED)), whole((1, PADDED))]
        + project_specs(layer)
        + [whole((32, tok)), whole((32, tok))],
        out_specs=(whole((WIDTH, tok)), whole((tok, 2 * KVD)), whole((tok, PADDED))),
        scratch_shapes=[pltpu.VMEM((WIDTH + 2 * KVD, tok), F32)],
        compiler_params=params(),
        cost_estimate=cost(2 * tok * 2048 * 1024, 5 << 20),
    )(stream, gain, weight, weight, cosine, sine)


def take_heads(ref, head):
    return jnp.concatenate(
        [ref[(GROUP * head + g) * HEAD : (GROUP * head + g + 1) * HEAD, :] for g in range(GROUP)],
        axis=1,
    )


def take_row(ref, head):
    return jnp.concatenate(
        [ref[GROUP * head + g : GROUP * head + g + 1, :] for g in range(GROUP)], axis=1
    )


def forward_kernel(
    range_ref, query_ref, packed_ref, bias_ref, mixed_ref, total_ref, top, total, mixed
):
    tok = query_ref.shape[1]
    top[...] = jnp.full(top.shape, MASKED, F32)
    total[...] = jnp.zeros(total.shape, F32)
    mixed[...] = jnp.zeros(mixed.shape, F32)

    def step(index, carry):
        rows = pl.ds(pl.multiple_of(index * CHUNK, CHUNK), CHUNK)
        bias = jnp.concatenate([bias_ref[rows, :]] * GROUP, axis=1)

        def scores_of(head):
            key = packed_ref[rows, head * HEAD : (head + 1) * HEAD]
            return nn_dot(key, take_heads(query_ref, head)) + bias

        later = scores_of(0)
        for head in range(KV_HEADS):
            scores = later
            if head + 1 < KV_HEADS:
                later = scores_of(head + 1)
            value = packed_ref[rows, KVD + head * HEAD : KVD + (head + 1) * HEAD]
            old_top = top[head]
            new_top = jnp.maximum(old_top, jnp.max(scores, axis=0, keepdims=True))
            raised = jnp.exp(scores - new_top)
            shrink = jnp.exp(old_top - new_top)
            top[head] = new_top
            total[head] = total[head] * shrink + jnp.sum(raised, axis=0, keepdims=True)
            mixed[head] = mixed[head] * shrink + tn_dot(value, raised.astype(BF16))
        return carry

    lax.fori_loop(range_ref[0], range_ref[1], step, 0)
    for head in range(KV_HEADS):
        result = mixed[head] / total[head]
        log_total = top[head] + jnp.log(total[head])
        for g in range(GROUP):
            at = GROUP * head + g
            columns = slice(g * tok, (g + 1) * tok)
            mixed_ref[at * HEAD : (at + 1) * HEAD, :] = result[:, columns]
            total_ref[at : at + 1, :] = log_total[:, columns]


def attend_forward(queries, packed, bias, chunk_range):
    tok = queries.shape[1]
    return pl.pallas_call(
        forward_kernel,
        out_shape=(shape((WIDTH, tok), F32), shape((HEADS, tok), F32)),
        in_specs=[IN_SMEM] + [IN_VMEM] * 3,
        out_specs=(IN_VMEM, IN_VMEM),
        scratch_shapes=[
            pltpu.VMEM((KV_HEADS, 1, GROUP * tok), F32),
            pltpu.VMEM((KV_HEADS, 1, GROUP * tok), F32),
            pltpu.VMEM((KV_HEADS, HEAD, GROUP * tok), F32),
        ],
        compiler_params=params(),
        cost_estimate=cost(4 * 4096 * 128 * 960, 8 << 20),
    )(chunk_range, queries, packed, bias)


def backward_kernel(
    range_ref,
    query_ref,
    packed_ref,
    bias_ref,
    total_ref,
    inner_ref,
    grad_ref,
    query_out,
    packed_out,
    grad_query,
):
    tok = query_ref.shape[1]
    packed_out[...] = jnp.zeros(packed_out.shape, packed_out.dtype)
    grad_query[...] = jnp.zeros(grad_query.shape, F32)

    def step(index, carry):
        rows = pl.ds(pl.multiple_of(index * CHUNK, CHUNK), CHUNK)
        bias = jnp.concatenate([bias_ref[rows, :]] * GROUP, axis=1)

        def products(head):
            key = packed_ref[rows, head * HEAD : (head + 1) * HEAD]
            value = packed_ref[rows, KVD + head * HEAD : KVD + (head + 1) * HEAD]
            scores = nn_dot(key, take_heads(query_ref, head)) + bias
            return key, scores, nn_dot(value, take_heads(grad_ref, head))

        later = products(0)
        for head in range(KV_HEADS):
            key, scores, grad_chance = later
            if head + 1 < KV_HEADS:
                later = products(head + 1)
            chance = jnp.exp(scores - take_row(total_ref, head))
            grad_scores = (chance * (grad_chance - take_row(inner_ref, head))).astype(BF16)
            grad_key = nt_dot(grad_scores, take_heads(query_ref, head)).astype(BF16)
            grad_value = nt_dot(chance.astype(BF16), take_heads(grad_ref, head)).astype(BF16)
            key_lanes = slice(head * HEAD, (head + 1) * HEAD)
            value_lanes = slice(KVD + head * HEAD, KVD + (head + 1) * HEAD)
            for block in range(CHUNK // tok):
                at = index * (CHUNK // tok // 2) + block // 2
                part = slice(block * tok, (block + 1) * tok)
                packed_out[block % 2, at, :, key_lanes] = grad_key[part, :]
                packed_out[block % 2, at, :, value_lanes] = grad_value[part, :]
            grad_query[head] += tn_dot(key, grad_scores)
        return carry

    lax.fori_loop(range_ref[0], range_ref[1], step, 0)
    for head in range(KV_HEADS):
        result = grad_query[head] * (1.0 / math.sqrt(HEAD))
        for g in range(GROUP):
            at = GROUP * head + g
            query_out[at * HEAD : (at + 1) * HEAD, :] = result[:, g * tok : (g + 1) * tok]


def attend_backward(queries, packed, bias, chunk_range, log_total, inner, grad_mixed):
    tok = queries.shape[1]
    return pl.pallas_call(
        backward_kernel,
        out_shape=(shape((WIDTH, tok), F32), shape((2, 16, tok, 2 * KVD), BF16)),
        in_specs=[IN_SMEM] + [IN_VMEM] * 6,
        out_specs=(IN_VMEM, IN_VMEM),
        scratch_shapes=[pltpu.VMEM((KV_HEADS, HEAD, GROUP * tok), F32)],
        compiler_params=params(),
        cost_estimate=cost(10 * 4096 * 128 * 960, 13 << 20),
    )(chunk_range, queries, packed, bias, log_total, inner, grad_mixed)


def feed_kernel(
    stream_ref, mixed_ref, gain_ref, output_ref, gate_w, up_w, contract_w, *rest
):
    mixed_out, middle_out, normed_out, gate_out, up_out, hidden_out, stream_out = rest
    tok = stream_ref.shape[0]

    @pl.when(pl.program_id(0) == 0)
    def _():
        pieces = []
        for dp in range(4):
            pieces += [mixed_ref[dp * 240 : dp * 240 + 240, :], jnp.zeros((16, tok), F32)]
        mixed = jnp.concatenate(pieces, axis=0).T.astype(BF16)
        mixed_out[...] = mixed
        middle = stream_ref[...] + nt_dot(mixed, tiles(output_ref, 32, 0, 32, 2, 0))
        middle_out[...] = middle
        normed_out[...] = (middle * norm_scale(middle) * gain_ref[...]).astype(BF16)
        stream_out[...] = middle

    normed = normed_out[...]
    gate = nt_dot(normed, tiles(gate_w, 4, 0, 160, 2, 0))
    up = nt_dot(normed, tiles(up_w, 4, 0, 160, 2, 0))
    gate_out[...] = gate
    up_out[...] = up
    hidden = (gate / (1.0 + jnp.exp(-gate)) * up).astype(BF16)
    hidden_out[...] = hidden
    stream_out[...] += nt_dot(hidden, tiles(contract_w, 32, 0, 32, 5, 0))


def whole(dims):
    return pl.BlockSpec(dims, lambda j: (0,) * len(dims))


def weight_specs(layer):
    return [
        pl.BlockSpec((4, 32, OUTPUT, 128), lambda j: (0, 0, 15 + layer, 0)),
        pl.BlockSpec((4, 4, EXPAND, 128), lambda j: (0, j, layer, 0)),
        pl.BlockSpec((4, 4, EXPAND, 128), lambda j: (0, j + 4, layer, 0)),
        pl.BlockSpec((1, 32, CONTRACT, 128), lambda j: (j, 0, 4 + layer, 0)),
    ]


def feed_forward(stream, mixed, gain, bulk, layer):
    tok = stream.shape[0]
    column = pl.BlockSpec((tok, 640), lambda j: (0, j))
    return pl.pallas_call(
        feed_kernel,
        grid=(4,),
        out_shape=(
            shape((tok, PADDED), BF16),
            shape((tok, PADDED), F32),
            shape((tok, PADDED), BF16),
            shape((tok, FF), F32),
            shape((tok, FF), F32),
            shape((tok, FF), BF16),
            shape((tok, PADDED), F32),
        ),
        in_specs=[whole((tok, PADDED)), whole((WIDTH, tok)), whole((1, PADDED))]
        + weight_specs(layer),
        out_specs=(whole((tok, PADDED)),) * 3 + (column,) * 3 + (whole((tok, PADDED)),),
        compiler_params=params(),
        cost_estimate=cost(2 * tok * 9000 * 1024, 18 << 20),
    )(stream, mixed, gain, bulk, bulk, bulk, bulk)


def feed_pull_kernel(
    grad_ref,
    middle_ref,
    gain_ref,
    mixed_ref,
    gate_ref,
    up_ref,
    output_ref,
    gate_w,
    up_w,
    contract_w,
    *rest,
):
    low_out, gate_up_out, middle_out, middle_low_out, gain_out, mixed_out, inner_out, total = rest
    index = pl.program_id(0)
    tok = grad_ref.shape[0]

    @pl.when(index == 0)
    def _():
        low_out[...] = grad_ref[...].astype(BF16)
        total[...] = jnp.zeros_like(total)

    gate, up = gate_ref[...], up_ref[...]
    grad_hidden = nn_dot(low_out[...], tiles(contract_w, 32, 0, 32, 5, 0))
    chance = 1.0 / (1.0 + jnp.exp(-gate))
    swish = gate * chance
    grad_gate = (grad_hidden * up * (chance + swish * (1.0 - chance))).astype(BF16)
    grad_up = (grad_hidden * swish).astype(BF16)
    gate_up_out[0] = grad_gate
    gate_up_out[1] = grad_up
    total[...] += nn_dot(grad_gate, tiles(gate_w, 4, 0, 160, 2, 0)) + nn_dot(
        grad_up, tiles(up_w, 4, 0, 160, 2, 0)
    )

    @pl.when(index == pl.num_programs(0) - 1)
    def _():
        grad_part, grad_gain = norm_pull(middle_ref[...], gain_ref[...], total[...])
        grad_middle = grad_ref[...] + grad_part
        middle_out[...] = grad_middle
        gain_out[...] = grad_gain
        low = grad_middle.astype(BF16)
        middle_low_out[...] = low
        back = nn_dot(low, tiles(output_ref, 32, 0, 32, 2, 0)).astype(BF16).astype(F32).T
        for dp in range(4):
            mixed_out[dp * 240 : dp * 240 + 240, :] = back[dp * 256 : dp * 256 + 240, :].astype(BF16)
        for head in range(HEADS):
            rows = slice(head * HEAD, head * HEAD + HEAD)
            product = mixed_out[rows, :].astype(F32) * mixed_ref[rows, :]
            inner_out[head : head + 1, :] = jnp.sum(product, axis=0, keepdims=True)


def feed_backward(grad, middle, gain, mixed, gate, up, bulk, layer):
    tok = grad.shape[0]
    column = pl.BlockSpec((tok, 640), lambda j: (0, j))
    return pl.pallas_call(
        feed_pull_kernel,
        grid=(4,),
        out_shape=(
            shape((tok, PADDED), BF16),
            shape((2, tok, FF), BF16),
            shape((tok, PADDED), F32),
            shape((tok, PADDED), BF16),
            shape((1, PADDED), F32),
            shape((WIDTH, tok), BF16),
            shape((HEADS, tok), F32),
        ),
        in_specs=[
            whole((tok, PADDED)),
            whole((tok, PADDED)),
            whole((1, PADDED)),
            whole((WIDTH, tok)),
            column,
            column,
        ]
        + weight_specs(layer),
        out_specs=(
            whole((tok, PADDED)),
            pl.BlockSpec((2, tok, 640), lambda j: (0, 0, j)),
            whole((tok, PADDED)),
            whole((tok, PADDED)),
            whole((1, PADDED)),
            whole((WIDTH, tok)),
            whole((HEADS, tok)),
        ),
        scratch_shapes=[pltpu.VMEM((tok, PADDED), F32)],
        compiler_params=params(),
        cost_estimate=cost(2 * tok * 9000 * 1024, 18 << 20),
    )(grad, middle, gain, mixed, gate, up, bulk, bulk, bulk, bulk)


def put_tiles(out_ref, result, rows, count, first):
    for dp in range(4):
        for tile in range(count):
            at = (dp * count + tile) * 128
            block = result[:, at : at + 128].reshape(4, rows, 128).astype(BF16)
            out_ref[:, dp, first + tile * rows : first + (tile + 1) * rows, :] = block


def weight_kernel(with_project, *refs):
    gate_ref, normed_ref, low_ref, hidden_ref, middle_ref, mixed_ref = refs[:6]
    out_ref = refs[-1]
    put_tiles(out_ref, tn_dot(gate_ref[0], normed_ref[...]), 160, 2, 0)
    put_tiles(out_ref, tn_dot(low_ref[...], hidden_ref[...]), 32, 5, EXPAND)
    put_tiles(out_ref, tn_dot(middle_ref[...], mixed_ref[...]), 32, 2, EXPAND + CONTRACT)
    if with_project:
        put_tiles(out_ref, nn_dot(refs[6][...], refs[7][...]), 64, 2, GRADS)


def weight_gradients(grad_gate_up, normed_feed, grad_low, hidden, middle_low, mixed, project):
    tok = normed_feed.shape[0]
    rows = GRADS + (PROJECT if project else 0)
    operands = [grad_gate_up, normed_feed, grad_low, hidden, middle_low, mixed]
    in_specs = [
        pl.BlockSpec((1, tok, 640), lambda j: (j // 4, 0, j % 4)),
        whole((tok, PADDED)),
        pl.BlockSpec((tok, 128), lambda j: (0, j)),
        whole((tok, FF)),
        pl.BlockSpec((tok, 128), lambda j: (0, j)),
        whole((tok, PADDED)),
    ]
    if project:
        operands += list(project)
        in_specs += [pl.BlockSpec((256, tok), lambda j: (j, 0)), whole((tok, PADDED))]
    return pl.pallas_call(
        functools.partial(weight_kernel, bool(project)),
        grid=(8,),
        out_shape=shape((32, 4, rows, 128), BF16),
        in_specs=in_specs,
        out_specs=pl.BlockSpec((4, 4, rows, 128), lambda j: (j, 0, 0, 0)),
        compiler_params=params(),
        cost_estimate=cost(2 * tok * 11000 * 1024, 20 << 20),
    )(*operands)


def project_pull_kernel(
    query_ref,
    local_ref,
    cosine_ref,
    sine_ref,
    weight_one,
    weight_two,
    stream_ref,
    gain_ref,
    grad_ref,
    *rest,
):
    padded_out, grad_out, gain_out, natural, spread = rest
    tok = stream_ref.shape[0]
    natural[0:WIDTH, :] = query_ref[...]
    natural[WIDTH : WIDTH + 2 * KVD, :] = local_ref[...].T
    cosine, sine = cosine_ref[...], sine_ref[...]
    for head in range(HEADS + KV_HEADS):
        at = head * HEAD
        first = natural[at : at + 32, :]
        second = natural[at + 32 : at + 64, :]
        natural[at : at + 32, :] = first * cosine + second * sine
        natural[at + 32 : at + 64, :] = second * cosine - first * sine
    for s in range(32):
        spread[s * 64 : s * 64 + 50, :] = natural[s * 50 : s * 50 + 50, :]
        spread[s * 64 + 50 : s * 64 + 64, :] = jnp.zeros((14, tok), F32)
    total = jnp.zeros((tok, PADDED), F32)
    for part in range(4):
        block = spread[part * 512 : (part + 1) * 512, :].astype(BF16)
        padded_out[part * 512 : (part + 1) * 512, :] = block
        total = total + tn_dot(block, project_tiles((weight_one, weight_two), part * 8))
    grad_part, grad_gain = norm_pull(stream_ref[...], gain_ref[...], total)
    grad_out[...] = grad_ref[...] + grad_part
    gain_out[...] = grad_gain


def project_backward(grad_query, grad_local, cosine, sine, weight, layer, stream, gain, grad_middle):
    tok = stream.shape[0]
    return pl.pallas_call(
        project_pull_kernel,
        grid=(1,),
        out_shape=(
            shape((2048, tok), BF16),
            shape((tok, PADDED), F32),
            shape((1, PADDED), F32),
        ),
        in_specs=[
            whole((WIDTH, tok)),
            whole((tok, 2 * KVD)),
            whole((32, tok)),
            whole((32, tok)),
        ]
        + project_specs(layer)
        + [whole((tok, PADDED)), whole((1, PADDED)), whole((tok, PADDED))],
        out_specs=(whole((2048, tok)), whole((tok, PADDED)), whole((1, PADDED))),
        scratch_shapes=[
            pltpu.VMEM((WIDTH + 2 * KVD, tok), F32),
            pltpu.VMEM((2048, tok), F32),
        ],
        compiler_params=params(),
        cost_estimate=cost(2 * tok * 2048 * 1024, 6 << 20),
    )(grad_query, grad_local, cosine, sine, weight, weight, stream, gain, grad_middle)


def lead_kernel(padded_ref, normed_ref, gains_ref, out_ref):
    result = nn_dot(padded_ref[...], normed_ref[...])
    for dp in range(4):
        for tile in range(2):
            at = (dp * 2 + tile) * 128
            block = result[:, at : at + 128].reshape(2, 2, 64, 128).astype(BF16)
            for core in range(2):
                out_ref[core, :, dp, tile * 64 : tile * 64 + 64, :] = block[:, core]
    for core in range(2):
        for place in range(2):
            out_ref[core, place, :, PROJECT:LEAD, :] = gains_ref[place * 2 + core]


def lead_gradients(padded, normed, gains):
    tok = normed.shape[0]
    return pl.pallas_call(
        lead_kernel,
        grid=(8,),
        out_shape=shape((2, 16, 4, LEAD, 128), BF16),
        in_specs=[
            pl.BlockSpec((256, tok), lambda j: (j, 0)),
            whole((tok, PADDED)),
            pl.BlockSpec((4, 4, LEAD - PROJECT, 128), lambda j: (j, 0, 0, 0)),
        ],
        out_specs=pl.BlockSpec((2, 2, 4, LEAD, 128), lambda j: (0, j, 0, 0, 0)),
        compiler_params=params(),
        cost_estimate=cost(2 * tok * 2048 * 1024, 6 << 20),
    )(padded, normed, gains)


def swap_cores(array):
    return lax.ppermute(array, "seq", SWAP)


def hop_y(array, hop):
    moves = [(i, i // 8 * 8 + (i % 8 + 2 * hop) % 8) for i in range(32)]
    return lax.ppermute(array, "seq", moves)


def hop_z(array, hop):
    return lax.ppermute(array, "seq", [(i, (i + 8 * hop) % 32) for i in range(32)])


def ring(array, move):
    return jnp.stack([array] + [move(array, hop) for hop in (1, 2, 3)])


def order_kernel(place_ref, first_own, last_own, first_other, last_other, out_ref):
    for s in range(32):
        back_z = lax.rem(place_ref[0] - s // 8 + 4, 4)
        back_y = lax.rem(place_ref[1] - s // 2 % 4 + 4, 4)
        same = place_ref[2] == s % 2

        @pl.when(same)
        def _(s=s, back_z=back_z, back_y=back_y):
            out_ref[s, 0] = first_own[back_z, back_y]
            out_ref[s, 1] = last_own[back_y, back_z]

        @pl.when(jnp.logical_not(same))
        def _(s=s, back_z=back_z, back_y=back_y):
            out_ref[s, 0] = first_other[back_z, back_y]
            out_ref[s, 1] = last_other[back_y, back_z]


def gather_seq(array):
    index = lax.axis_index("seq")
    first = ring(array[0], hop_y)
    last = ring(array[1], hop_z)
    first = ring(first, hop_z)
    last = ring(last, hop_y)
    place = jnp.stack([index // 8, index // 2 % 4, index % 2]).astype(jnp.int32)
    return pl.pallas_call(
        order_kernel,
        out_shape=shape((32,) + array.shape, array.dtype),
        in_specs=[IN_SMEM] + [IN_VMEM] * 4,
        out_specs=IN_VMEM,
        compiler_params=params(),
        cost_estimate=cost(0, 12 << 20),
    )(place, first, last, swap_cores(first), swap_cores(last))


def reduce_seq(array):
    core = lax.axis_index("seq") % 2
    mine = lax.dynamic_index_in_dim(array, core, 0, keepdims=False)
    theirs = lax.dynamic_index_in_dim(array, 1 - core, 0, keepdims=False)
    arrived = swap_cores(theirs)
    both = (mine.astype(F32) + arrived.astype(F32)).astype(BF16)
    spread = lax.all_to_all(both, "seq", 0, 0, axis_index_groups=PLANE, tiled=True)
    return jnp.sum(spread.astype(F32), axis=0)


def ring_sum(array, place, move):
    total = lax.dynamic_index_in_dim(array, place, 0, keepdims=False).astype(F32)
    for hop in (1, 2, 3):
        block = lax.dynamic_index_in_dim(array, (place + hop) % 4, 0, keepdims=False)
        total = total + move(block, hop).astype(F32)
    return total


def reduce_packed(array):
    index = lax.axis_index("seq")
    core, along_y, along_z = index % 2, index // 2 % 4, index // 8
    rows, width = array.shape[2] // 2, array.shape[3]
    mine = lax.dynamic_index_in_dim(array, core, 0, keepdims=False)
    theirs = lax.dynamic_index_in_dim(array, 1 - core, 0, keepdims=False)
    both = mine.astype(F32) + swap_cores(theirs).astype(F32)
    both = both.astype(BF16).reshape(4, 4, 2, rows, width)
    first = both[:, :, 0]
    last = both[:, :, 1].transpose(1, 0, 2, 3)
    first = ring_sum(first, along_z, hop_z).astype(BF16)
    last = ring_sum(last, along_y, hop_y).astype(BF16)
    first = ring_sum(first, along_y, hop_y)
    last = ring_sum(last, along_z, hop_z)
    return jnp.concatenate([first, last], axis=0)


def reduce_dp(array):
    array = array.astype(BF16)
    place = lax.axis_index("dp")
    total = lax.dynamic_index_in_dim(array, place, 0, keepdims=False).astype(F32)
    for hop in (1, 2, 3):
        block = lax.dynamic_index_in_dim(array, (place + hop) % 4, 0, keepdims=False)
        moved = lax.ppermute(block, "dp", [(i, (i + hop) % 4) for i in range(4)])
        total = total + moved.astype(F32)
    return total


def pad_last(array, size):
    return jnp.pad(array, [(0, 0)] * (array.ndim - 1) + [(0, size - array.shape[-1])])


def pad_groups(array):
    groups = array.reshape(array.shape[:-1] + (array.shape[-1] // 30, 30))
    return pad_last(groups, 32).reshape(array.shape[:-1] + (-1,))


def drop_groups(array):
    groups = array.reshape(array.shape[:-1] + (array.shape[-1] // 32, 32))
    return groups[..., :30].reshape(array.shape[:-1] + (-1,))


def to_tiles(array, rows):
    array = jnp.pad(array, ((0, rows - array.shape[0]), (0, 0)))
    count = array.shape[1] // 128
    return array.reshape(rows, count, 128).transpose(1, 0, 2).reshape(count * rows, 128)


def from_tiles(array, rows):
    count = array.shape[0] // rows
    return array.reshape(count, rows, 128).transpose(1, 0, 2).reshape(rows, count * 128)


def on_device(inputs, w_project, w_output, w_expand, w_contract, norm_gains, segments, cotangent):
    tok = inputs.shape[1]
    layers = 2
    local_segment = segments[0]

    pieces = [to_tiles(pad_groups(w_expand[layer].T), 160) for layer in range(layers)]
    pieces += [to_tiles(w_contract[layer].T, 32) for layer in range(layers)]
    pieces += [to_tiles(pad_last(w_output[layer].T, 256), 32) for layer in range(layers)]
    pieces += [to_tiles(pad_groups(w_project[1].T), 64)]
    bulk = lax.all_gather(jnp.concatenate(pieces, axis=0), ("dp", "seq"))
    bulk = bulk.reshape((4, 32) + bulk.shape[1:])

    extra = jnp.zeros((LEAD - PROJECT - 2, 128), BF16)
    lead = jnp.concatenate(
        [
            to_tiles(pad_groups(w_project[0].T), 64),
            pad_last(norm_gains[None, :], 128),
            local_segment.astype(BF16)[None, :],
            extra,
        ],
        axis=0,
    )
    leads = lax.all_gather(lead, "dp").reshape(2, 2, LEAD, 128)
    leads = gather_seq(leads).reshape(32, 4, LEAD, 128)
    gains = leads[:, :, PROJECT, :32].transpose(1, 0, 2).reshape(4, 1, PADDED).astype(F32)
    all_segment = lax.dynamic_index_in_dim(
        leads[:, :, PROJECT + 1, :], lax.axis_index("dp"), 1, keepdims=False
    )
    all_segment = all_segment.reshape(-1).astype(jnp.int32)
    length = all_segment.shape[0]
    projects = [leads, bulk]

    query_index = lax.axis_index("seq") * tok + jnp.arange(tok, dtype=jnp.int32)
    key_index = jnp.arange(length, dtype=jnp.int32)
    starts = jnp.sum((all_segment[:, None] < local_segment[None, :]).astype(jnp.int32), axis=0)
    position = (query_index - starts).astype(F32)
    angle = frequencies(HEAD)[:, None] * position[None, :]
    cosine = jnp.cos(angle)
    sine = jnp.sin(angle)
    allowed = (local_segment[None, :] == all_segment[:, None]) & (
        query_index[None, :] >= key_index[:, None]
    )
    bias = jnp.where(allowed, 0.0, MASKED).astype(F32)
    chunk_range = jnp.stack([starts[0] // CHUNK, query_index[-1] // CHUNK + 1])

    stream = pad_groups(inputs[0]).astype(F32)
    records = []
    for layer in range(layers):
        queries, packed_local, normed = project_forward(
            stream, gains[2 * layer], projects[layer], layer, cosine, sine
        )
        packed = gather_seq(packed_local.reshape(2, tok // 2, 2 * KVD)).reshape(length, 2 * KVD)
        mixed_wide, log_total = attend_forward(queries, packed, bias, chunk_range)
        mixed, middle, normed_feed, gate, up, hidden, after = feed_forward(
            stream, mixed_wide, gains[2 * layer + 1], bulk, layer
        )
        records.append(
            (stream, queries, packed, normed, mixed_wide, log_total)
            + (mixed, middle, normed_feed, gate, up, hidden)
        )
        stream = after
    block_output = drop_groups(stream.astype(BF16))[None]

    grad_stream = pad_groups(cotangent[0]).astype(F32)
    gain_grads = [None] * 4
    bulk_grads = [None] * layers
    project = None
    for layer in reversed(range(layers)):
        stream_in, queries, packed, normed, mixed_wide, log_total = records[layer][:6]
        mixed, middle, normed_feed, gate, up, hidden = records[layer][6:]
        grad_low, grad_gate_up, grad_middle, middle_low, gain_grad, grad_mixed, inner = (
            feed_backward(
                grad_stream, middle, gains[2 * layer + 1], mixed_wide, gate, up, bulk, layer
            )
        )
        gain_grads[2 * layer + 1] = gain_grad
        payload = weight_gradients(
            grad_gate_up, normed_feed, grad_low, hidden, middle_low, mixed, project
        )
        bulk_grads[layer] = lax.psum_scatter(payload, "seq", scatter_dimension=0)
        grad_query, grad_packed = attend_backward(
            queries, packed, bias, chunk_range, log_total, inner, grad_mixed
        )
        grad_local = reduce_packed(grad_packed)
        padded, grad_stream, gain_grad = project_backward(
            grad_query,
            grad_local,
            cosine,
            sine,
            projects[layer],
            layer,
            stream_in,
            gains[2 * layer],
            grad_middle,
        )
        gain_grads[2 * layer] = gain_grad
        project = (padded, normed)

    gain_rows = jnp.concatenate(gain_grads, axis=0).astype(BF16).reshape(4, 32, 32)
    gain_rows = gain_rows.transpose(1, 0, 2)[:, :, None, :]
    gain_rows = jnp.pad(gain_rows, ((0, 0), (0, 0), (0, LEAD - PROJECT - 1), (0, 96)))
    second = reduce_dp(bulk_grads[1])
    lead_grads, second = lax.optimization_barrier(
        (lead_gradients(padded, normed, gain_rows), second)
    )
    lead_part = reduce_dp(reduce_seq(lead_grads))
    first = reduce_dp(bulk_grads[0])
    parts = [first, second]
    last_part = first[GRADS:]

    def project_out(tile_rows):
        return drop_groups(from_tiles(tile_rows, 64)[:50]).T

    expand_out = jnp.stack([drop_groups(from_tiles(part[:EXPAND], 160)).T for part in parts])
    contract_out = jnp.stack(
        [from_tiles(part[EXPAND : EXPAND + CONTRACT], 32)[:30].T for part in parts]
    )
    output_out = jnp.stack(
        [from_tiles(part[EXPAND + CONTRACT : GRADS], 32)[:30, :240].T for part in parts]
    )
    return (
        block_output,
        drop_groups(grad_stream)[None],
        jnp.stack([project_out(lead_part[:PROJECT]), project_out(last_part)]),
        output_out,
        expand_out,
        contract_out,
        lead_part[PROJECT, :30],
    )


def solution(mesh):
    in_specs = (
        P("dp", "seq", None),
        P(None, "dp", "seq"),
        P(None, "dp", "seq"),
        P(None, "dp", "seq"),
        P(None, "dp", "seq"),
        P(("dp", "seq")),
        P("dp", "seq"),
        P("dp", "seq", None),
    )
    out_specs = (
        P("dp", "seq", None),
        P("dp", "seq", None),
        P(None, "dp", "seq"),
        P(None, "dp", "seq"),
        P(None, "dp", "seq"),
        P(None, "dp", "seq"),
        P(("dp", "seq")),
    )
    return jax.shard_map(
        on_device, mesh=mesh, in_specs=in_specs, out_specs=out_specs, check_vma=False
    )
```
